128 devices in a mesh: obs: 16 (over y, z), emis: 8 (over x, core).
Axes of the slice: x: 4, y: 4, z: 4, core: 2. Of those that a mesh axis runs over, the one named last changes fastest.
Arguments:
- control: float32 [2048, 256, 128], P(('obs', 'emis')), may hold values from -6 to 6
- prior_flux: float32 [2048, 256], P(('obs', 'emis')), may hold values from 0.1 to 3
- correlation: float32 [256, 256], replicated, may hold values from -0.375 to 0.375
- footprints: bfloat16 [512, 24, 256, 256], P(('obs', 'emis')), may hold values from -0.078125 to 0.078125
- obs_values: float32 [131072, 128], P(('obs', 'emis')), may hold values from -6 to 6
- obs_weights: float32 [131072], P(('obs', 'emis')), may hold values from 0.2 to 5
- tile_ids: int32 [512, 24], P(('obs', 'emis')), may hold values from 0 to 2047, as said below
Outputs:
- gradient: float32 [2048, 256, 128], P(('obs', 'emis'))
The draws below stay inside these ranges and needn't reach their ends.
Inputs may be any that keep to these rules, and one draw needn't show every extreme that they name: `tile_ids`: tile t is owned by the device of index t // 16, counting obs slowest. The 96 tiles touched by the blocks of one device are all distinct and name each owner device at most 1 times; one owner, the same for every device, is named exactly 1 times by every device.
All inputs are finite; a program needn't handle non-finite values.
Results may differ from the reference program's by a relative error of at most 0.0041.
Values may be sent and summed in bfloat16 or wider, within the bound.
A program may use at most 128 MiB of HBM per device.

```python
import math
import jax
import jax.numpy as jnp
from jax import lax

TS = 256
NB = 256
MEM = 128
K = 24
TILE_DEV = 16
BLK_DEV = 4
OWNERS = 128
CAP = 1
TILES = 2048
OBS_BLOCKS = 512
OBS = 131072


def draw_tile_ids(key, part):
    key = jax.random.fold_in(key, 11)
    hot_owner = jax.random.randint(jax.random.fold_in(key, 1), (), 0, OWNERS)
    wanted = BLK_DEV * K
    slot_owner = jnp.arange(OWNERS * CAP, dtype=jnp.int32) // CAP
    slot_rank = jnp.arange(OWNERS * CAP, dtype=jnp.int32) % CAP

    def one_source(source):
        sub_key = jax.random.fold_in(key, source + 2)
        key_order, key_base, key_shuffle = jax.random.split(sub_key, 3)
        priority = jnp.where(slot_owner == hot_owner, -1, jax.random.permutation(key_order, OWNERS * CAP).astype(jnp.int32))
        chosen = jnp.argsort(priority, stable=True)[:wanted]
        base_tile = jax.random.randint(key_base, (OWNERS,), 0, TILE_DEV)
        owner_pick = slot_owner[chosen]
        local_tile = (base_tile[owner_pick] + slot_rank[chosen]) % TILE_DEV
        tile_list = owner_pick * TILE_DEV + local_tile
        return jax.random.permutation(key_shuffle, tile_list).astype(jnp.int32)
    every = jax.vmap(one_source)(jnp.arange(OWNERS, dtype=jnp.int32))
    return every.reshape(OBS_BLOCKS, K)


def steps_of(own_key, shape, shards, least, largest):
    level, own = 1.0, jax.random.fold_in(own_key, 6)
    for dim, blocks in shards:
        steps = jnp.exp(jax.random.uniform(jax.random.fold_in(own, dim), (blocks,), jnp.float32, least / len(shards), largest / len(shards)))
        level = level * jnp.repeat(steps, shape[dim] // blocks).reshape([-1 if axis == dim else 1 for axis in range(len(shape))])
    return level


def centred(stream_key, extent, deviation, most, cuts=(), kind=jnp.bfloat16):
    entries = deviation * jax.random.normal(stream_key, extent, jnp.float32)
    if cuts:
        entries = entries * steps_of(stream_key, extent, cuts, -0.22, 0.18)
    return jnp.clip(entries, -most, most).astype(kind)


def setup_inputs(seed: int = 0) -> dict:
    arg_keys = jax.random.split(jax.random.key(seed), 8)
    control = centred(arg_keys[0], (TILES, TS, MEM), 1.0, 6.0, ((0, 128),), jnp.float32)
    prior_flux = jnp.clip(jnp.exp(math.log(3.0) - 3.4011974 * jax.random.uniform(arg_keys[1], (TILES, TS), jnp.float32) ** steps_of(arg_keys[1], (TILES, TS), ((0, 128),), -0.2, 0.2)), 0.1, 3.0)
    correlation = centred(arg_keys[2], (TS, TS), TS ** -0.5, 0.375, (), jnp.float32)
    footprints = centred(arg_keys[3], (OBS_BLOCKS, K, NB, TS), (K * TS) ** -0.5, 0.078125, ((0, 128),))
    obs_values = centred(arg_keys[4], (OBS, MEM), 1.0, 6.0, ((0, 128),), jnp.float32)
    obs_weights = jnp.clip(jnp.exp(math.log(5.0) - 3.218876 * jax.random.uniform(arg_keys[5], (OBS,), jnp.float32) ** steps_of(arg_keys[5], (OBS,), ((0, 128),), -0.2, 0.2)), 0.2, 5.0)
    tile_ids = draw_tile_ids(jax.random.fold_in(arg_keys[7], 71), 0)
    return {"control": control, "prior_flux": prior_flux, "correlation": correlation, "footprints": footprints, "obs_values": obs_values, "obs_weights": obs_weights, "tile_ids": tile_ids}


def reference(control, prior_flux, correlation, footprints, obs_values, obs_weights, tile_ids):
    emission = prior_flux[:, :, None] + jnp.einsum("ct,ntm->ncm", correlation, control, precision=lax.Precision.HIGHEST)
    emission_bf = emission.astype(jnp.bfloat16)
    observed = obs_values.reshape(OBS_BLOCKS, NB, MEM)
    weights = obs_weights.reshape(OBS_BLOCKS, NB)

    def one_block(adjoint, inputs):
        footprint, tile_list, values, weight_row = inputs
        tiles_in = emission_bf[tile_list.astype(jnp.int32)]
        foot_wide = footprint.astype(jnp.float32)
        modeled = jnp.einsum("kot,ktm->om", foot_wide, tiles_in.astype(jnp.float32), precision=lax.Precision.HIGHEST)
        mismatch = ((modeled - values) * weight_row[:, None]).astype(jnp.bfloat16)
        partial_value = jnp.einsum("kot,om->ktm", foot_wide, mismatch.astype(jnp.float32), precision=lax.Precision.HIGHEST).astype(jnp.bfloat16)
        adjoint = adjoint.at[tile_list.astype(jnp.int32)].add(partial_value.astype(jnp.float32))
        return adjoint, None

    start = jnp.zeros((TILES, TS, MEM), jnp.float32)
    adjoint, unused = lax.scan(one_block, start, (footprints, tile_ids, observed, weights))
    return control + jnp.einsum("ct,ncm->ntm", correlation, adjoint, precision=lax.Precision.HIGHEST)
```

```python
import functools

import jax
import jax.numpy as jnp
from jax import lax
from jax.experimental import pallas as pl
from jax.experimental.pallas import tpu as pltpu
from jax.sharding import PartitionSpec as P

MESH = pl.DeviceIdType.MESH
BF = jnp.bfloat16
F32 = jnp.float32
I32 = jnp.int32
VMEM_BYTES = 60 * 2**20

ORDERS = ((0, 1, 2), (1, 2, 0), (2, 0, 1))


def part_rows(cells):
    third = cells // 48 * 16
    return (cells - 2 * third, third, third)


def steps_of(n):
    return [k for k in (1, 3, 2) if k < n]


def here(n):
    o, e = lax.axis_index("obs"), lax.axis_index("emis")
    return (lax.div(e, 2), lax.div(o, n), lax.rem(o, n)), lax.rem(e, 2)


def device_of(n, xyz, core):
    return (xyz[1] * n + xyz[2], xyz[0] * 2 + core)


def owner_of(n, xyz, core):
    return ((xyz[1] * n + xyz[2]) * n + xyz[0]) * 2 + core


def moved(n, xyz, axis, k):
    return tuple(lax.rem(v + k, n) if a == axis else v for a, v in enumerate(xyz))


def placed(xyz, axis, value):
    return tuple(value if a == axis else v for a, v in enumerate(xyz))


def remote(src, dst, send, recv, device):
    copy = pltpu.make_async_remote_copy(
        src_ref=src, dst_ref=dst, send_sem=send, recv_sem=recv, device_id=device, device_id_type=MESH
    )
    copy.start()
    return copy


def enter(n, xyz, core):
    barrier = pltpu.get_barrier_semaphore()
    count = 0
    for axis in range(3):
        for k in range(1, n):
            for dc in range(2):
                target = device_of(n, moved(n, xyz, axis, k), lax.rem(core + dc, 2))
                pl.semaphore_signal(barrier, inc=1, device_id=target, device_id_type=MESH)
                count += 1
    pl.semaphore_signal(barrier, inc=1, device_id=device_of(n, xyz, 1 - core), device_id_type=MESH)
    pl.semaphore_wait(barrier, count + 1)


def split(value):
    high = value.astype(BF)
    return high, (value - high.astype(F32)).astype(BF)


def dot(a, b):
    return jnp.dot(a, b, preferred_element_type=F32)


def column(row):
    return jnp.broadcast_to(row, (row.shape[1], row.shape[1])).T


def forward_kernel(
    n, rows, ids_ref, control_ref, prior_ref, corr_ref, foot_hbm, obs_ref, weight_ref,
    mm_ref, pair_ref, prev_ref, last_ref,
    g00, g01, g02, g03, g10, g11, g12, g13, g20, g21, g22, g23,
    s0, s1, s2, b0, b1, b2, a0, a1, a2,
    foot, mine, row_ids, table, table_t, table_s,
    foot_sem, id_send, id_recv, table_sem, one_send, one_recv, two_send, two_recv, last_send, last_recv, keep_sem,
):
    gathered = ((g00, g01, g02, g03), (g10, g11, g12, g13), (g20, g21, g22, g23))
    picked, middle, arrived = (s0, s1, s2), (b0, b1, b2), (a0, a1, a2)
    tiles, cells, members = control_ref.shape
    blocks, touched = ids_ref.shape
    xyz, core = here(n)
    steps = steps_of(n)
    starts = (0, rows[0], rows[0] + rows[1])
    lanes = 2 * n * n * n

    load_foot = pltpu.make_async_copy(foot_hbm, foot, foot_sem)
    load_foot.start()

    lane = lax.broadcasted_iota(I32, (8, lanes), 1)
    wanted = jnp.full((8, lanes), tiles, I32)
    pair = jnp.zeros((8, lanes), I32)
    for b in range(blocks):
        for k in range(touched):
            tile = ids_ref[b, k]
            match = lane == lax.div(tile, tiles)
            wanted = jnp.where(match, lax.rem(tile, tiles), wanted)
            pair = jnp.where(match, b * touched + k, pair)
    pair_ref[...] = pair
    mine[...] = wanted
    me = xyz[0] * 2 + core
    row_ids[pl.ds(me, 1)] = wanted[None]

    enter(n, xyz, core)

    sent = []
    row_copies = []
    for dx in range(n):
        for dc in range(2):
            if dx or dc:
                target = device_of(n, moved(n, xyz, 0, dx), lax.rem(core + dc, 2))
                i = dx * 2 + dc
                row_copies.append(remote(mine, row_ids.at[me], id_send.at[i], id_recv.at[i], target))
    sent += row_copies

    corr_h, corr_l = split(corr_ref[...])
    one = {}
    halves = 2
    half = tiles // halves
    for h in range(halves):

        def emit(i, carry, h=h):
            t = h * half + 2 * i
            both = jnp.concatenate([control_ref[t], control_ref[t + 1]], axis=1)
            both_h, both_l = split(both)
            flux = dot(corr_h, both_h) + (dot(corr_h, both_l) + dot(corr_l, both_h))
            for u in range(2):
                prior = prior_ref[pl.ds(t + u, 1), :]
                base = jnp.concatenate(
                    [column(prior[:, members * v : members * (v + 1)]) for v in range(cells // members)], axis=0
                )
                tile = (base + flux[:, members * u : members * (u + 1)]).astype(BF)
                for p in range(3):
                    gathered[p][0][t + u] = tile[starts[p] : starts[p] + rows[p]]
            return carry

        lax.fori_loop(0, half // 2, emit, 0)
        for k in steps:
            for p, order in enumerate(ORDERS):
                i = (p * n + k) * halves + h
                span = pl.ds(h * half, half)
                one[p, k, h] = remote(
                    gathered[p][0].at[span], gathered[p][n - k].at[span], one_send.at[i], one_recv.at[i],
                    device_of(n, moved(n, xyz, order[0], k), core),
                )
                sent.append(one[p, k, h])

    for copy in row_copies:
        copy.wait_recv()
    for e in range(2 * n):
        table[xyz[2], xyz[1], e : e + 1, :] = row_ids[e, 0:1, :]
    at = 2 * n
    copies = []
    for k in steps:
        copies.append(
            remote(table.at[xyz[2], xyz[1]], table.at[xyz[2], xyz[1]], id_send.at[at + k], id_recv.at[at + k],
                   device_of(n, moved(n, xyz, 1, k), core))
        )
    for copy in copies:
        copy.wait_recv()
    sent += copies
    at += n
    copies = []
    for k in steps:
        copies.append(
            remote(table.at[xyz[2]], table.at[xyz[2]], id_send.at[at + k], id_recv.at[at + k],
                   device_of(n, moved(n, xyz, 2, k), core))
        )
    for copy in copies:
        copy.wait_recv()
    sent += copies
    to_scalar = pltpu.make_async_copy(table, table_s, table_sem)
    to_scalar.start()
    to_scalar.wait()

    two = {}
    for j in [0] + steps:
        for p, (first, second, third) in enumerate(ORDERS):
            if j:
                for h in range(halves):
                    one[p, n - j, h].wait_recv()
            source = lax.rem(xyz[first] + j, n)
            owner = owner_of(n, placed(xyz, first, source), core)
            slot = xyz[second] * n + source
            for kk, k in enumerate(steps + [0]):
                column_at = moved(n, xyz, second, k)

                def pick(d, carry, p=p, j=j, k=k, kk=kk, third=third, column_at=column_at, owner=owner, slot=slot):
                    x, y, z = placed(column_at, third, lax.div(d, 2))
                    tile = table_s[z, y, x * 2 + lax.rem(d, 2), owner]
                    value = gathered[p][j][jnp.minimum(tile, tiles - 1)]
                    if k:
                        picked[p][kk, j, d] = value
                    else:
                        middle[p][d, slot] = value
                    return carry

                lax.fori_loop(0, 2 * n, pick, 0)
                if k:
                    i = (p * n + k) * n + j
                    two[p, k, j] = remote(
                        picked[p].at[kk, j], middle[p].at[:, slot], two_send.at[i], two_recv.at[i],
                        device_of(n, column_at, core),
                    )
                    sent.append(two[p, k, j])

    final = []
    kept = []
    for k in [0] + steps:
        if k:
            for p in range(3):
                for j in range(n):
                    two[p, k, j].wait_recv()
        for ds in steps + [0]:
            for dc in range(2):
                for p, (first, second, third) in enumerate(ORDERS):
                    source = lax.rem(xyz[second] + n - k, n)
                    span = pl.ds(source * n, n)
                    mine_at = xyz[third] * 2 + core
                    if ds or dc:
                        goal = moved(n, xyz, third, ds)
                        goal_core = lax.rem(core + dc, 2)
                        i = ((p * n + k) * n + ds) * 2 + dc
                        copy = remote(
                            middle[p].at[goal[third] * 2 + goal_core, span], arrived[p].at[mine_at, span],
                            last_send.at[i], last_recv.at[i], device_of(n, goal, goal_core),
                        )
                        final.append(copy)
                    else:
                        copy = pltpu.make_async_copy(
                            middle[p].at[mine_at, span], arrived[p].at[mine_at, span], keep_sem.at[p * n + k]
                        )
                        copy.start()
                        kept.append(copy)
    sent += final

    flat = table[...].reshape(lanes, lanes)
    table_t[...] = flat.T
    shape = (lanes, lanes)
    coords = []
    for dim in range(2):
        r = lax.broadcasted_iota(I32, shape, dim)
        coords.append(
            ((lax.div(lax.rem(r, 2 * n), 2), lax.rem(lax.div(r, 2 * n), n), lax.div(r, 2 * n * n)), lax.rem(r, 2))
        )
    none = 2 * n * n
    tile_at = lax.broadcasted_iota(I32, (tiles, lanes), 0).astype(F32)
    last_lane = lax.broadcasted_iota(I32, (tiles, lanes), 1)
    lasts = jnp.full((tiles, lanes), float(none), F32)
    prev_ref[...] = jnp.zeros(prev_ref.shape, I32)
    for p, (first, second, third) in enumerate(ORDERS):
        rank = [((c[second] * n + c[third]) * 2 + o).astype(F32) for c, o in coords]
        in_plane = [c[first] == xyz[first] for c, o in coords]
        earlier = (rank[0] < rank[1]) & in_plane[0]
        for j in range(n):
            owner = owner_of(n, moved(n, xyz, first, j), core)
            across = jnp.broadcast_to(table_t[pl.ds(owner, 1), :].astype(F32), shape)
            down = across.T
            before = jnp.max(jnp.where(earlier & (across == down), rank[0], -1.0), axis=0, keepdims=True)
            before = jnp.where(before < 0, float(none), before)
            prev_ref[p * n + j : p * n + j + 1, :] = before.astype(I32)
            hit = (across[:tiles] == tile_at) & in_plane[1][:tiles]
            newest = jnp.max(jnp.where(hit, rank[1][:tiles], -1.0), axis=1, keepdims=True)
            newest = jnp.where(newest < 0, float(none), newest)
            lasts = jnp.where(last_lane == p * n + j, newest, lasts)
    last_ref[...] = lasts.astype(I32)

    load_foot.wait()
    for copy in kept:
        copy.wait()
    for copy in final:
        copy.wait_recv()

    per_block = foot.shape[1]
    for b in range(blocks):

        def add(k, total, b=b):
            tile = lax.div(ids_ref[b, k], tiles)
            oc = lax.rem(tile, 2)
            x = lax.rem(lax.div(tile, 2), n)
            z = lax.rem(lax.div(tile, 2 * n), n)
            y = lax.div(tile, 2 * n * n)
            c = (x, y, z)
            flux = jnp.concatenate(
                [
                    arrived[p][c[third] * 2 + oc, c[second] * n + c[first]]
                    for p, (first, second, third) in enumerate(ORDERS)
                ],
                axis=0,
            )
            return total + dot(foot[b * touched + k], flux)

        modeled = lax.fori_loop(0, touched, add, jnp.zeros((per_block, members), F32), unroll=4)
        per = per_block // members
        weight = jnp.concatenate([column(weight_ref[b * per + v : b * per + v + 1, :]) for v in range(per)], axis=0)
        mm_ref[b] = ((modeled - obs_ref[b * per_block : (b + 1) * per_block, :]) * weight).astype(BF)

    for copy in sent:
        copy.wait_send()


def backward_kernel(
    n, rows, touched, pair_ref, prev_ref, last_ref, mm_ref, control_ref, corr_ref, foot_hbm,
    out_ref,
    p0, p1, p2, b0, b1, b2, c0, c1, c2, h0, h1, h2, q0, q1, q2, r0, r1, r2, o0, o1, o2,
    foot,
    foot_sem, last_send, last_recv, keep_sem, two_send, two_recv, hold_sem, one_send, one_recv,
):
    partial, middle, back, chain = (p0, p1, p2), (b0, b1, b2), (c0, c1, c2), (h0, h1, h2)
    outgoing, incoming, own = (q0, q1, q2), (r0, r1, r2), (o0, o1, o2)
    tiles, cells, members = control_ref.shape
    xyz, core = here(n)
    x, y, z = xyz
    steps = steps_of(n)
    starts = (0, rows[0], rows[0] + rows[1])
    none = 2 * n * n

    load_foot = pltpu.make_async_copy(foot_hbm, foot, foot_sem)
    load_foot.start()
    for p in range(3):
        chain[p][none] = jnp.zeros((rows[p], members), F32)
    enter(n, xyz, core)
    load_foot.wait()

    sent = []
    one_way = {}
    for kz in steps + [0]:
        zo = lax.rem(z + kz, n)

        def make(i, carry, zo=zo):
            oc, xo, yo = lax.rem(i, 2), lax.rem(lax.div(i, 2), n), lax.div(i, 2 * n)
            pair = pair_ref[0, owner_of(n, (xo, yo, zo), oc)]
            value = lax.dot_general(
                foot[pair], mm_ref[lax.div(pair, touched)], (((0,), (0,)), ((), ())), preferred_element_type=F32
            ).astype(BF)
            c = (xo, yo, zo)
            for p, (first, second, third) in enumerate(ORDERS):
                partial[p][c[third] * 2 + oc, c[second], c[first]] = value[starts[p] : starts[p] + rows[p]]
            return carry

        lax.fori_loop(0, 2 * n * n, make, 0, unroll=2)
        for ds in steps + [0]:
            for dc in range(2):
                for p, (first, second, third) in enumerate(ORDERS):
                    if third == 2:
                        if ds != steps[0]:
                            continue
                        ds_here = kz
                        view = lambda ref, block: ref.at[block]
                    elif second == 2:
                        ds_here = ds
                        view = lambda ref, block: ref.at[block, zo]
                    else:
                        ds_here = ds
                        view = lambda ref, block: ref.at[block, :, zo]
                    mine_at = xyz[third] * 2 + core
                    i = ((p * n + kz) * n + ds_here) * 2 + dc
                    if ds_here or dc:
                        goal = moved(n, xyz, third, ds_here)
                        goal_core = lax.rem(core + dc, 2)
                        copy = remote(
                            view(partial[p], goal[third] * 2 + goal_core), view(middle[p], mine_at),
                            last_send.at[i], last_recv.at[i], device_of(n, goal, goal_core),
                        )
                        sent.append(copy)
                    else:
                        copy = pltpu.make_async_copy(
                            view(partial[p], mine_at), view(middle[p], mine_at), keep_sem.at[p * n + kz]
                        )
                        copy.start()
                    one_way.setdefault((p, kz), []).append((copy, bool(ds_here or dc)))

    def arrive(p, kz):
        for copy, far in one_way[p, kz]:
            if far:
                copy.wait_recv()
            else:
                copy.wait()

    two = {}

    def pass_on(p, k, j):
        first, second, third = ORDERS[p]
        goal = moved(n, xyz, second, k)
        to = goal[second]
        row = lax.rem(xyz[first] + j, n)
        src, dst = middle[p].at[:, to, row], back[p].at[row, xyz[second]]
        i = (p * n + k) * n + j
        if k:
            two[p, k, j] = remote(src, dst, two_send.at[i], two_recv.at[i], device_of(n, goal, core))
            sent.append(two[p, k, j])
        else:
            two[p, k, j] = pltpu.make_async_copy(src, dst, hold_sem.at[p * n + j])
            two[p, k, j].start()

    for kz in steps + [0]:
        for p, (first, second, third) in enumerate(ORDERS):
            if second == 2:
                arrive(p, kz)
                for j in steps + [0]:
                    pass_on(p, kz, j)
            elif first == 2:
                arrive(p, kz)
                for k in steps + [0]:
                    pass_on(p, k, kz)
    for p, (first, second, third) in enumerate(ORDERS):
        if third == 2:
            for kz in steps + [0]:
                arrive(p, kz)
            for j in steps + [0]:
                for k in steps + [0]:
                    pass_on(p, k, j)

    one = {}
    for jj, j in enumerate(steps + [0]):
        for p in (1, 2, 0):
            first, second, third = ORDERS[p]
            for k in steps:
                two[p, k, j].wait_recv()
            two[p, 0, j].wait()
            row = lax.rem(xyz[first] + j, n)

            def link(s, carry, p=p, j=j, row=row, first=first, second=second, third=third):
                so, d = lax.div(s, 2 * n), lax.rem(s, 2 * n)
                c = placed(placed(xyz, second, so), third, lax.div(d, 2))
                device = (c[2] * n + c[1]) * (2 * n) + c[0] * 2 + lax.rem(d, 2)
                before = prev_ref[p * n + j, device]
                chain[p][s] = back[p][row, so, d].astype(F32) + chain[p][before]
                return carry

            lax.fori_loop(0, none, link, 0)

            def collect(t, carry, p=p, j=j, jj=jj):
                total = chain[p][last_ref[t, p * n + j]]
                if j:
                    outgoing[p][jj, t] = total.astype(BF)
                else:
                    own[p][t] = total
                return carry

            lax.fori_loop(0, tiles, collect, 0)
            if j:
                i = p * n + j
                one[p, j] = remote(
                    outgoing[p].at[jj], incoming[p].at[jj], one_send.at[i], one_recv.at[i],
                    device_of(n, moved(n, xyz, first, j), core),
                )
                sent.append(one[p, j])

    for copy in one.values():
        copy.wait_recv()

    corr_h, corr_l = split(corr_ref[...].T)

    def finish(i, carry):
        t = 2 * i
        sums = []
        for u in range(2):
            sums.append(
                jnp.concatenate(
                    [
                        own[p][t + u] + sum(incoming[p][jj, t + u].astype(F32) for jj in range(n - 1))
                        for p in range(3)
                    ],
                    axis=0,
                )
            )
        both_h, both_l = split(jnp.concatenate(sums, axis=1))
        spread = dot(corr_h, both_h) + (dot(corr_h, both_l) + dot(corr_l, both_h))
        for u in range(2):
            out_ref[t + u] = control_ref[t + u] + spread[:, members * u : members * (u + 1)]
        return carry

    lax.fori_loop(0, tiles // 2, finish, 0)

    for copy in sent:
        copy.wait_send()


def per_device(n, control, prior_flux, correlation, footprints, obs_values, obs_weights, tile_ids):
    tiles, cells, members = control.shape
    blocks, touched = tile_ids.shape
    per_block = footprints.shape[2]
    owners = 2 * n * n * n
    rows = part_rows(cells)
    foot = footprints.reshape(blocks * touched, per_block, cells)
    vmem, smem, anywhere = (
        pl.BlockSpec(memory_space=pltpu.VMEM),
        pl.BlockSpec(memory_space=pltpu.SMEM),
        pl.BlockSpec(memory_space=pl.ANY),
    )
    dma = pltpu.SemaphoreType.DMA
    foot_scratch = pltpu.VMEM((blocks * touched, per_block, cells), BF)
    mm, pair, prev, last = pl.pallas_call(
        functools.partial(forward_kernel, n, rows),
        name="forward",
        out_shape=(
            jax.ShapeDtypeStruct((blocks, per_block, members), BF),
            jax.ShapeDtypeStruct((8, owners), I32),
            jax.ShapeDtypeStruct((16, owners), I32),
            jax.ShapeDtypeStruct((tiles, owners), I32),
        ),
        in_specs=[smem, vmem, vmem, vmem, anywhere, vmem, vmem],
        out_specs=(vmem,) * 4,
        scratch_shapes=(
            [pltpu.VMEM((tiles, r, members), BF) for r in rows for _ in range(4)]
            + [pltpu.VMEM((n - 1, n, 2 * n, r, members), BF) for r in rows]
            + [pltpu.VMEM((2 * n, n * n, r, members), BF) for r in rows]
            + [pltpu.VMEM((2 * n, n * n, r, members), BF) for r in rows]
            + [
                foot_scratch,
                pltpu.VMEM((8, owners), I32),
                pltpu.VMEM((2 * n, 8, owners), I32),
                pltpu.VMEM((n, n, 2 * n, owners), I32),
                pltpu.VMEM((owners, owners), I32),
                pltpu.SMEM((n, n, 2 * n, owners), I32),
                dma(()), dma((4 * n,)), dma((4 * n,)), dma(()),
                dma((6 * n,)), dma((6 * n,)),
                dma((3 * n * n,)), dma((3 * n * n,)),
                dma((6 * n * n,)), dma((6 * n * n,)),
                dma((3 * n,)),
            ]
        ),
        compiler_params=pltpu.CompilerParams(
            collective_id=0, has_side_effects=True, vmem_limit_bytes=VMEM_BYTES
        ),
    )(tile_ids, control, prior_flux, correlation, foot, obs_values, obs_weights.reshape(-1, members))
    return pl.pallas_call(
        functools.partial(backward_kernel, n, rows, touched),
        name="backward",
        out_shape=jax.ShapeDtypeStruct(control.shape, F32),
        in_specs=[smem, smem, smem, vmem, vmem, vmem, anywhere],
        out_specs=vmem,
        scratch_shapes=(
            [pltpu.VMEM((2 * n, n, n, r, members), BF) for r in rows]
            + [pltpu.VMEM((2 * n, n, n, r, members), BF) for r in rows]
            + [pltpu.VMEM((n, n, 2 * n, r, members), BF) for r in rows]
            + [pltpu.VMEM((2 * n * n + 1, r, members), F32) for r in rows]
            + [pltpu.VMEM((n - 1, tiles, r, members), BF) for r in rows]
            + [pltpu.VMEM((n - 1, tiles, r, members), BF) for r in rows]
            + [pltpu.VMEM((tiles, r, members), F32) for r in rows]
            + [
                foot_scratch,
                dma(()),
                dma((6 * n * n,)), dma((6 * n * n,)), dma((3 * n,)),
                dma((3 * n * n,)), dma((3 * n * n,)), dma((3 * n,)),
                dma((3 * n,)), dma((3 * n,)),
            ]
        ),
        compiler_params=pltpu.CompilerParams(
            collective_id=1, has_side_effects=True, vmem_limit_bytes=VMEM_BYTES
        ),
    )(pair, prev, last, mm, control, correlation, foot)


def solution(mesh):
    n = mesh.shape["emis"] // 2
    return jax.shard_map(
        functools.partial(per_device, n),
        mesh=mesh,
        in_specs=(
            P(("obs", "emis"), None, None),
            P(("obs", "emis"), None),
            P(),
            P(("obs", "emis"), None, None, None),
            P(("obs", "emis"), None),
            P(("obs", "emis")),
            P(("obs", "emis"), None),
        ),
        out_specs=P(("obs", "emis"), None, None),
        check_vma=False,
    )
```

```python
import functools

import jax
import jax.numpy as jnp
from jax import lax
from jax.experimental import pallas as pl
from jax.experimental.pallas import tpu as pltpu
from jax.sharding import PartitionSpec as P

MESH = pl.DeviceIdType.MESH
BF = jnp.bfloat16
F32 = jnp.float32
I32 = jnp.int32
VMEM_BYTES = 60 * 2**20

ORDERS = ((0, 1, 2), (1, 2, 0), (2, 0, 1))


def part_rows(cells):
    third = cells // 48 * 16
    return (cells - 2 * third, third, third)


STEPS = (1, 3, 2)
BACK = (2, 1, 3)


def here(n):
    o, e = lax.axis_index("obs"), lax.axis_index("emis")
    return (lax.div(e, 2), lax.div(o, n), lax.rem(o, n)), lax.rem(e, 2)


def device_of(n, xyz, core):
    return (xyz[1] * n + xyz[2], xyz[0] * 2 + core)


def owner_of(n, xyz, core):
    return ((xyz[1] * n + xyz[2]) * n + xyz[0]) * 2 + core


def moved(n, xyz, axis, k):
    return tuple(lax.rem(v + k, n) if a == axis else v for a, v in enumerate(xyz))


def placed(xyz, axis, value):
    return tuple(value if a == axis else v for a, v in enumerate(xyz))


def remote(src, dst, send, recv, device):
    copy = pltpu.make_async_remote_copy(
        src_ref=src, dst_ref=dst, send_sem=send, recv_sem=recv, device_id=device, device_id_type=MESH
    )
    copy.start()
    return copy


def line_partners(n, xyz, core):
    for axis in range(3):
        for k in range(1, n):
            for dc in range(2):
                yield device_of(n, moved(n, xyz, axis, k), lax.rem(core + dc, 2))
    yield device_of(n, xyz, 1 - core)


def partners(n, xyz, core):
    yield from line_partners(n, xyz, core)
    for dy in range(1, n):
        for dz in range(1, n):
            yield device_of(n, moved(n, moved(n, xyz, 1, dy), 2, dz), core)


def split(value):
    high = value.astype(BF)
    return high, (value - high.astype(F32)).astype(BF)


def dot(a, b):
    return jnp.dot(a, b, preferred_element_type=F32)


def column(row):
    return jnp.broadcast_to(row, (row.shape[1], row.shape[1])).T


def kernel(
    n, rows, ids_ref, prior_ref, corr_ref, weight_ref, control_hbm, foot_hbm, obs_hbm,
    out_hbm,
    g00, g01, g02, g03, g10, g11, g12, g13, g20, g21, g22, g23,
    s0, s1, s2, b0, b1, b2, a0, a1, a2, h0, h1, h2, r0, r1, r2, m0, m1, m2, o0, o1, o2,
    foot, control, obs, out, mismatch, mine, row_ids, table, table_t, pair_v, prev_v, last_v,
    table_s, pair_s, prev_s, last_s,
    load_sem, id_send, id_recv, scalar_sem, one_send, one_recv, two_send, two_recv, three_send, three_recv, keep_sem,
    back_three_send, back_three_recv, back_keep_sem, back_two_send, back_two_recv, back_one_send, back_one_recv,
    out_sem, free_sem,
):
    gathered = ((g00, g01, g02, g03), (g10, g11, g12, g13), (g20, g21, g22, g23))
    picked, middle, arrived = (s0, s1, s2), (b0, b1, b2), (a0, a1, a2)
    chain, sums_in, relay, own = (h0, h1, h2), (r0, r1, r2), (m0, m1, m2), (o0, o1, o2)
    tiles, cells, members = control.shape
    blocks, touched = ids_ref.shape
    per_block = foot.shape[1]
    xyz, core = here(n)
    starts = (0, rows[0], rows[0] + rows[1])
    lanes = 2 * n * n * n
    none = 2 * n * n
    half = tiles // 2
    halves = (pl.ds(0, half), pl.ds(half, half))

    barrier = pltpu.get_barrier_semaphore()
    count = 0
    for target in partners(n, xyz, core):
        pl.semaphore_signal(barrier, inc=1, device_id=target, device_id_type=MESH)
        count += 1

    loads = []
    for i, (src, dst) in enumerate(((control_hbm, control), (foot_hbm, foot), (obs_hbm, obs))):
        loads.append(pltpu.make_async_copy(src, dst, load_sem.at[i]))
        loads[-1].start()
    load_control, load_foot, load_obs = loads

    lane = lax.broadcasted_iota(I32, (8, lanes), 1)
    wanted = jnp.full((8, lanes), tiles, I32)
    pair = jnp.zeros((8, lanes), I32)
    for b in range(blocks):
        for k in range(touched):
            tile = ids_ref[b, k]
            match = lane == lax.div(tile, tiles)
            wanted = jnp.where(match, lax.rem(tile, tiles), wanted)
            pair = jnp.where(match, b * touched + k, pair)
    pair_v[...] = pair
    mine[...] = wanted
    me = xyz[0] * 2 + core
    row_ids[pl.ds(me, 1)] = wanted[None]
    to_scalar = [pltpu.make_async_copy(pair_v, pair_s, scalar_sem.at[0])]
    to_scalar[0].start()

    corr_h, corr_l = split(corr_ref[...])
    load_control.wait()

    def emit(i, carry):
        t = 2 * i
        both = jnp.concatenate([control[t], control[t + 1]], axis=1)
        both_h, both_l = split(both)
        flux = dot(corr_h, both_h) + (dot(corr_h, both_l) + dot(corr_l, both_h))
        for u in range(2):
            prior = prior_ref[pl.ds(t + u, 1), :]
            base = jnp.concatenate(
                [column(prior[:, members * v : members * (v + 1)]) for v in range(cells // members)], axis=0
            )
            tile = (base + flux[:, members * u : members * (u + 1)]).astype(BF)
            for p in range(3):
                gathered[p][0][t + u] = tile[starts[p] : starts[p] + rows[p]]
        return carry

    lax.fori_loop(0, tiles // 2, emit, 0)

    pl.semaphore_wait(barrier, count)

    sent = []
    row_copies = []
    for dx in range(n):
        for dc in range(2):
            if dx or dc:
                target = device_of(n, moved(n, xyz, 0, dx), lax.rem(core + dc, 2))
                i = dx * 2 + dc
                row_copies.append(remote(mine, row_ids.at[me], id_send.at[i], id_recv.at[i], target))
    sent += row_copies

    one = {}

    def gather(p, k, j, h):
        i = (p * n + (j - k) % n) * 2 + h
        one[p, (j - k) % n, h] = remote(
            gathered[p][j].at[halves[h]], gathered[p][(j - k) % n].at[halves[h]], one_send.at[i], one_recv.at[i],
            device_of(n, moved(n, xyz, ORDERS[p][0], k), core),
        )
        sent.append(one[p, (j - k) % n, h])

    for p in range(3):
        gather(p, 3, 0, 0)
        gather(p, 1, 0, 1)

    for copy in row_copies:
        copy.wait_recv()
    for e in range(2 * n):
        table[xyz[2], xyz[1], e : e + 1, :] = row_ids[e, 0:1, :]
    plane_copies = []
    at = 2 * n
    for dy in range(n):
        for dz in range(n):
            if dy or dz:
                target = device_of(n, moved(n, moved(n, xyz, 1, dy), 2, dz), core)
                i = at + dy * n + dz
                here_ids = table.at[xyz[2], xyz[1]]
                plane_copies.append(remote(here_ids, here_ids, id_send.at[i], id_recv.at[i], target))
    sent += plane_copies

    for p in range(3):
        gather(p, 3, 0, 1)
        gather(p, 1, 0, 0)
    for p in range(3):
        one[p, 1, 0].wait_recv()
        gather(p, 3, 1, 0)
        one[p, 3, 1].wait_recv()
        gather(p, 1, 3, 1)

    for copy in plane_copies:
        copy.wait_recv()
    table_copy = pltpu.make_async_copy(table, table_s, scalar_sem.at[1])
    table_copy.start()
    table_copy.wait()

    two = {}
    for j in (0,) + STEPS:
        for p, (first, second, third) in enumerate(ORDERS):
            if j == 2:
                one[p, 2, 0].wait_recv()
                one[p, 2, 1].wait_recv()
            elif j:
                one[p, j, 1 if j == 1 else 0].wait_recv()
            source = lax.rem(xyz[first] + j, n)
            owner = owner_of(n, placed(xyz, first, source), core)
            for kk, k in enumerate(STEPS + (0,)):
                column_at = moved(n, xyz, second, k)

                def pick(d, carry, p=p, j=j, k=k, kk=kk, third=third, column_at=column_at, owner=owner, source=source,
                         second=second):
                    x, y, z = placed(column_at, third, lax.div(d, 2))
                    tile = table_s[z, y, x * 2 + lax.rem(d, 2), owner]
                    value = gathered[p][j][jnp.clip(tile, 0, tiles - 1)]
                    if k:
                        picked[p][kk, j, d] = value
                    else:
                        middle[p][d, xyz[second], source] = value
                    return carry

                lax.fori_loop(0, 2 * n, pick, 0)
                if k:
                    i = (p * n + k) * n + j
                    two[p, k, j] = remote(
                        picked[p].at[kk, j], middle[p].at[:, xyz[second], source], two_send.at[i], two_recv.at[i],
                        device_of(n, column_at, core),
                    )
                    sent.append(two[p, k, j])

    final = []
    kept = []
    for k in (0,) + STEPS:
        if k:
            for p in range(3):
                for j in range(n):
                    two[p, k, j].wait_recv()
        for ds in STEPS + (0,):
            for dc in range(2):
                for p, (first, second, third) in enumerate(ORDERS):
                    source = lax.rem(xyz[second] + n - k, n)
                    mine_at = xyz[third] * 2 + core
                    if ds or dc:
                        goal = moved(n, xyz, third, ds)
                        goal_core = lax.rem(core + dc, 2)
                        i = ((p * n + k) * n + ds) * 2 + dc
                        copy = remote(
                            middle[p].at[goal[third] * 2 + goal_core, source], arrived[p].at[mine_at, source],
                            three_send.at[i], three_recv.at[i], device_of(n, goal, goal_core),
                        )
                        final.append(copy)
                    else:
                        copy = pltpu.make_async_copy(
                            middle[p].at[mine_at, source], arrived[p].at[mine_at, source], keep_sem.at[p * n + k]
                        )
                        copy.start()
                        kept.append(copy)
    sent += final

    table_t[...] = table[...].reshape(lanes, lanes).T
    shape = (lanes, lanes)
    coords = []
    for dim in range(2):
        r = lax.broadcasted_iota(I32, shape, dim)
        coords.append(
            ((lax.div(lax.rem(r, 2 * n), 2), lax.rem(lax.div(r, 2 * n), n), lax.div(r, 2 * n * n)), lax.rem(r, 2))
        )
    tile_at = lax.broadcasted_iota(I32, (tiles, lanes), 0)
    last_lane = lax.broadcasted_iota(I32, (tiles, lanes), 1)
    lasts = jnp.full((tiles, lanes), none, I32)
    prev_v[...] = jnp.zeros(prev_v.shape, I32)
    for p, (first, second, third) in enumerate(ORDERS):
        rank = [
            (lax.rem(c[second] + (n - xyz[second]), n) * n + c[third]) * 2 + o for c, o in coords
        ]
        in_plane = [c[first] == xyz[first] for c, o in coords]
        earlier = (rank[0] < rank[1]) & in_plane[0]
        for j in range(n):
            owner = owner_of(n, moved(n, xyz, first, j), core)
            across = jnp.broadcast_to(table_t[pl.ds(owner, 1), :], shape)
            down = across.T
            before = jnp.max(jnp.where(earlier & (across == down), rank[0], -1), axis=0, keepdims=True)
            prev_v[p * n + j : p * n + j + 1, :] = jnp.where(before < 0, none, before)
            hit = (across[:tiles] == tile_at) & in_plane[1][:tiles]
            newest = jnp.max(jnp.where(hit, rank[1][:tiles], -1), axis=1, keepdims=True)
            newest = jnp.where(newest < 0, none, newest)
            lasts = jnp.where(last_lane == p * n + j, newest, lasts)
    last_v[...] = lasts
    for i, (src, dst) in enumerate(((prev_v, prev_s), (last_v, last_s))):
        to_scalar.append(pltpu.make_async_copy(src, dst, scalar_sem.at[2 + i]))
        to_scalar[-1].start()
    for p in range(3):
        chain[p][none] = jnp.zeros((rows[p], members), F32)

    load_foot.wait()
    load_obs.wait()
    for copy in to_scalar + kept:
        copy.wait()
    for copy in final:
        copy.wait_recv()
    for copy in sent:
        copy.wait_send()
    freed = 0
    for target in line_partners(n, xyz, core):
        pl.semaphore_signal(free_sem, inc=1, device_id=target, device_id_type=MESH)
        freed += 1

    per = per_block // members

    def model(b, carry):
        feet, flux = [], []
        for k in range(touched):
            tile = lax.div(ids_ref[b, k], tiles)
            oc = lax.rem(tile, 2)
            c = (lax.rem(lax.div(tile, 2), n), lax.div(tile, 2 * n * n), lax.rem(lax.div(tile, 2 * n), n))
            for p, (first, second, third) in enumerate(ORDERS):
                flux.append(arrived[p][c[third] * 2 + oc, c[second], c[first]])
            feet.append(foot[b * touched + k])
        modeled = dot(jnp.concatenate(feet, axis=1), jnp.concatenate(flux, axis=0))
        weight = jnp.concatenate([column(weight_ref[pl.ds(b * per + v, 1), :]) for v in range(per)], axis=0)
        wrong = (modeled - obs[pl.ds(pl.multiple_of(b * per_block, per_block), per_block), :]) * weight
        mismatch[b] = wrong.T.astype(BF)
        return carry

    lax.fori_loop(0, blocks, model, 0)

    sent = []
    one_way = {}
    for kz in BACK + (0,):
        zo = lax.rem(xyz[2] + kz, n)

        def make(i, carry, zo=zo):
            oc, xo, yo = lax.rem(i, 2), lax.rem(lax.div(i, 2), n), lax.div(i, 2 * n)
            pair = jnp.clip(pair_s[0, owner_of(n, (xo, yo, zo), oc)], 0, blocks * touched - 1)
            value = dot(mismatch[lax.div(pair, touched)], foot[pair]).astype(BF).T
            c = (xo, yo, zo)
            for p, (first, second, third) in enumerate(ORDERS):
                arrived[p][c[third] * 2 + oc, c[second], c[first]] = value[starts[p] : starts[p] + rows[p]]
            return carry

        lax.fori_loop(0, 2 * n * n, make, 0, unroll=4)
        if kz == BACK[0]:
            pl.semaphore_wait(free_sem, freed)
        for ds in STEPS + (0,):
            for dc in range(2):
                for p, (first, second, third) in enumerate(ORDERS):
                    if third == 2:
                        if ds != STEPS[0]:
                            continue
                        step = kz
                        view = lambda ref, block: ref.at[block]
                    elif second == 2:
                        step = ds
                        view = lambda ref, block: ref.at[block, zo]
                    else:
                        step = ds
                        view = lambda ref, block: ref.at[block, :, zo]
                    mine_at = xyz[third] * 2 + core
                    i = ((p * n + kz) * n + step) * 2 + dc
                    far = bool(step or dc)
                    if far:
                        goal = moved(n, xyz, third, step)
                        goal_core = lax.rem(core + dc, 2)
                        copy = remote(
                            view(arrived[p], goal[third] * 2 + goal_core), view(middle[p], mine_at),
                            back_three_send.at[i], back_three_recv.at[i], device_of(n, goal, goal_core),
                        )
                        sent.append(copy)
                    else:
                        copy = pltpu.make_async_copy(
                            view(arrived[p], mine_at), view(middle[p], mine_at), back_keep_sem.at[p * n + kz]
                        )
                        copy.start()
                    one_way.setdefault((p, kz), []).append((copy, far))

    def arrive(p, kz):
        for copy, far in one_way[p, kz]:
            if far:
                copy.wait_recv()
            else:
                copy.wait()

    two = {}

    def pass_on(p, k, j):
        first, second, third = ORDERS[p]
        if not k:
            return
        goal = moved(n, xyz, second, k)
        row = lax.rem(xyz[first] + j, n)
        i = (p * n + k) * n + j
        two[p, k, j] = remote(
            middle[p].at[:, goal[second], row], picked[p].at[STEPS.index(n - k), j],
            back_two_send.at[i], back_two_recv.at[i], device_of(n, goal, core),
        )
        sent.append(two[p, k, j])

    for kz in BACK + (0,):
        for p, (first, second, third) in enumerate(ORDERS):
            if second == 2:
                arrive(p, kz)
                for j in BACK + (0,):
                    pass_on(p, kz, j)
            elif first == 2:
                arrive(p, kz)
                for k in STEPS:
                    pass_on(p, k, kz)
    for p, (first, second, third) in enumerate(ORDERS):
        if third == 2:
            for kz in BACK + (0,):
                arrive(p, kz)
            for j in BACK + (0,):
                for k in STEPS:
                    pass_on(p, k, j)

    one = {}
    relayed = {}

    def give(p, k, j, h, key, src, dst, i):
        copy = remote(
            src, dst, back_one_send.at[i], back_one_recv.at[i],
            device_of(n, moved(n, xyz, ORDERS[p][0], k), core),
        )
        sent.append(copy)
        return copy

    for j in (2, 0, 1, 3):
        for p in (1, 2, 0):
            first, second, third = ORDERS[p]
            for k in STEPS:
                two[p, k, j].wait_recv()
            row = lax.rem(xyz[first] + j, n)
            for step in (0, 1, 2, 3):

                def link(d, carry, p=p, j=j, row=row, first=first, second=second, third=third, step=step):
                    so = lax.rem(xyz[second] + step, n)
                    c = placed(placed(xyz, second, so), third, lax.div(d, 2))
                    device = (c[2] * n + c[1]) * (2 * n) + c[0] * 2 + lax.rem(d, 2)
                    before = jnp.clip(prev_s[p * n + j, device], 0, none)
                    if step:
                        value = picked[p][STEPS.index(step), j, d]
                    else:
                        value = middle[p][d, so, row]
                    chain[p][step * 2 * n + d] = value.astype(F32) + chain[p][before]
                    return carry

                lax.fori_loop(0, 2 * n, link, 0)

            for h in range(2):
                joins = (j == 1 and h == 0) or (j == 3 and h == 1)
                if joins:
                    relayed[p, h].wait_recv()

                def collect(t, carry, p=p, j=j, h=h, joins=joins):
                    total = chain[p][jnp.clip(last_s[h * half + t, p * n + j], 0, none)]
                    if joins:
                        total = total + relay[p][h, t].astype(F32)
                    if j:
                        gathered[p][j][h * half + t] = total.astype(BF)
                    else:
                        own[p][h * half + t] = total
                    return carry

                lax.fori_loop(0, half, collect, 0)
                if j == 2:
                    k = 1 if h == 0 else 3
                    relayed[p, h] = give(
                        p, k, j, h, "relay", gathered[p][j].at[halves[h]], relay[p].at[h], (p * n + 2) * 2 + h
                    )
                elif j:
                    one[p, j, h] = give(
                        p, j, j, h, "sum", gathered[p][j].at[halves[h]],
                        sums_in[p].at[0 if j == 1 else 1, halves[h]], (p * n + j) * 2 + h,
                    )

    corr_h, corr_l = split(corr_ref[...].T)
    stores = []
    for h in range(2):
        for p in (1, 2, 0):
            for j in (1, 3):
                one[p, j, h].wait_recv()

        def finish(i, carry, h=h):
            t = h * half + 2 * i
            adjoint = []
            for u in range(2):
                adjoint.append(
                    jnp.concatenate(
                        [
                            own[p][t + u] + (sums_in[p][0, t + u].astype(F32) + sums_in[p][1, t + u].astype(F32))
                            for p in range(3)
                        ],
                        axis=0,
                    )
                )
            both_h, both_l = split(jnp.concatenate(adjoint, axis=1))
            spread = dot(corr_h, both_h) + (dot(corr_h, both_l) + dot(corr_l, both_h))
            for u in range(2):
                out[t + u] = control[t + u] + spread[:, members * u : members * (u + 1)]
            return carry

        lax.fori_loop(0, half // 2, finish, 0)
        stores.append(pltpu.make_async_copy(out.at[halves[h]], out_hbm.at[halves[h]], out_sem.at[h]))
        stores[-1].start()

    for copy in sent:
        copy.wait_send()
    for copy in stores:
        copy.wait()


def per_device(n, control, prior_flux, correlation, footprints, obs_values, obs_weights, tile_ids):
    tiles, cells, members = control.shape
    blocks, touched = tile_ids.shape
    per_block = footprints.shape[2]
    owners = 2 * n * n * n
    rows = part_rows(cells)
    foot = footprints.reshape(blocks * touched, per_block, cells)
    vmem, smem, anywhere = (
        pl.BlockSpec(memory_space=pltpu.VMEM),
        pl.BlockSpec(memory_space=pltpu.SMEM),
        pl.BlockSpec(memory_space=pl.ANY),
    )

    def dma(count):
        return pltpu.SemaphoreType.DMA((count,))

    return pl.pallas_call(
        functools.partial(kernel, n, rows),
        name="gradient",
        out_shape=jax.ShapeDtypeStruct(control.shape, F32),
        in_specs=[smem, vmem, vmem, vmem, anywhere, anywhere, anywhere],
        out_specs=anywhere,
        scratch_shapes=(
            [pltpu.VMEM((tiles, r, members), BF) for r in rows for _ in range(4)]
            + [pltpu.VMEM((n - 1, n, 2 * n, r, members), BF) for r in rows]
            + [pltpu.VMEM((2 * n, n, n, r, members), BF) for r in rows]
            + [pltpu.VMEM((2 * n, n, n, r, members), BF) for r in rows]
            + [pltpu.VMEM((2 * n * n + 1, r, members), F32) for r in rows]
            + [pltpu.VMEM((2, tiles, r, members), BF) for r in rows]
            + [pltpu.VMEM((2, tiles // 2, r, members), BF) for r in rows]
            + [pltpu.VMEM((tiles, r, members), F32) for r in rows]
            + [
                pltpu.VMEM((blocks * touched, per_block, cells), BF),
                pltpu.VMEM(control.shape, F32),
                pltpu.VMEM(obs_values.shape, F32),
                pltpu.VMEM(control.shape, F32),
                pltpu.VMEM((blocks, members, per_block), BF),
                pltpu.VMEM((8, owners), I32),
                pltpu.VMEM((2 * n, 8, owners), I32),
                pltpu.VMEM((n, n, 2 * n, owners), I32),
                pltpu.VMEM((owners, owners), I32),
                pltpu.VMEM((8, owners), I32),
                pltpu.VMEM((16, owners), I32),
                pltpu.VMEM((tiles, owners), I32),
                pltpu.SMEM((n, n, 2 * n, owners), I32),
                pltpu.SMEM((8, owners), I32),
                pltpu.SMEM((16, owners), I32),
                pltpu.SMEM((tiles, owners), I32),
                dma(3), dma(2 * n + n * n), dma(2 * n + n * n), dma(4),
                dma(6 * n), dma(6 * n),
                dma(3 * n * n), dma(3 * n * n),
                dma(6 * n * n), dma(6 * n * n), dma(3 * n),
                dma(6 * n * n), dma(6 * n * n), dma(3 * n),
                dma(3 * n * n), dma(3 * n * n),
                dma(6 * n), dma(6 * n),
                dma(2), pltpu.SemaphoreType.REGULAR,
            ]
        ),
        compiler_params=pltpu.CompilerParams(
            collective_id=0, has_side_effects=True, vmem_limit_bytes=VMEM_BYTES
        ),
    )(tile_ids, prior_flux, correlation, obs_weights.reshape(-1, members), control, foot, obs_values)


def solution(mesh):
    n = mesh.shape["emis"] // 2
    return jax.shard_map(
        functools.partial(per_device, n),
        mesh=mesh,
        in_specs=(
            P(("obs", "emis"), None, None),
            P(("obs", "emis"), None),
            P(),
            P(("obs", "emis"), None, None, None),
            P(("obs", "emis"), None),
            P(("obs", "emis")),
            P(("obs", "emis"), None),
        ),
        out_specs=P(("obs", "emis"), None, None),
        check_vma=False,
    )
```

```python
import functools

import jax
import jax.numpy as jnp
from jax import lax
from jax.experimental import pallas as pl
from jax.experimental.pallas import tpu as pltpu
from jax.sharding import PartitionSpec as P

MESH = pl.DeviceIdType.MESH
BF = jnp.bfloat16
F32 = jnp.float32
I32 = jnp.int32
VMEM_BYTES = 60 * 2**20

ORDERS = ((0, 1, 2), (1, 2, 0), (2, 0, 1))


SHARED = 16


def part_starts(cells):
    third = cells // 48 * 16
    return (0, third, cells - third)


def part_rows(cells):
    third = cells // 48 * 16
    return (third + SHARED, third + SHARED, third)


def sent_rows(rows, p, other):
    if p == 0 and other:
        return pl.ds(0, rows[0] - SHARED)
    if p == 1 and not other:
        return pl.ds(SHARED, rows[1] - SHARED)
    return pl.ds(0, rows[p])


STEPS = (1, 3, 2)
BACK = (2, 1, 3)


def here(n):
    o, e = lax.axis_index("obs"), lax.axis_index("emis")
    return (lax.div(e, 2), lax.div(o, n), lax.rem(o, n)), lax.rem(e, 2)


def device_of(n, xyz, core):
    return (xyz[1] * n + xyz[2], xyz[0] * 2 + core)


def owner_of(n, xyz, core):
    return ((xyz[1] * n + xyz[2]) * n + xyz[0]) * 2 + core


def moved(n, xyz, axis, k):
    return tuple(lax.rem(v + k, n) if a == axis else v for a, v in enumerate(xyz))


def placed(xyz, axis, value):
    return tuple(value if a == axis else v for a, v in enumerate(xyz))


def remote(src, dst, send, recv, device):
    copy = pltpu.make_async_remote_copy(
        src_ref=src, dst_ref=dst, send_sem=send, recv_sem=recv, device_id=device, device_id_type=MESH
    )
    copy.start()
    return copy


def line_partners(n, xyz, core):
    for axis in range(3):
        for k in range(1, n):
            for dc in range(2):
                yield device_of(n, moved(n, xyz, axis, k), lax.rem(core + dc, 2))
    yield device_of(n, xyz, 1 - core)


def partners(n, xyz, core):
    yield from line_partners(n, xyz, core)
    for dy in range(1, n):
        for dz in range(1, n):
            yield device_of(n, moved(n, moved(n, xyz, 1, dy), 2, dz), core)


def split(value):
    high = value.astype(BF)
    return high, (value - high.astype(F32)).astype(BF)


def dot(a, b):
    return jnp.dot(a, b, preferred_element_type=F32)


def column(row):
    return jnp.broadcast_to(row, (row.shape[1], row.shape[1])).T


def kernel(
    n, rows, ids_ref, prior_ref, corr_ref, weight_ref, control_hbm, foot_hbm, obs_hbm,
    out_hbm,
    g00, g01, g02, g03, g10, g11, g12, g13, g20, g21, g22, g23,
    s0, s1, s2, b0, b1, b2, a0, a1, a2, h0, h1, h2, r0, r1, r2, m0, m1, m2, o0, o1, o2,
    foot, control, obs, out, mismatch, mine, row_ids, table, table_t, pair_v, prev_v, last_v,
    table_s, pair_s, prev_s, last_s,
    load_sem, id_send, id_recv, scalar_sem, one_send, one_recv, two_send, two_recv, three_send, three_recv, keep_sem,
    back_three_send, back_three_recv, back_keep_sem, back_two_send, back_two_recv, back_one_send, back_one_recv,
    out_sem, free_sem,
):
    gathered = ((g00, g01, g02, g03), (g10, g11, g12, g13), (g20, g21, g22, g23))
    picked, middle, arrived = (s0, s1, s2), (b0, b1, b2), (a0, a1, a2)
    chain, sums_in, relay, own = (h0, h1, h2), (r0, r1, r2), (m0, m1, m2), (o0, o1, o2)
    tiles, cells, members = control.shape
    blocks, touched = ids_ref.shape
    per_block = foot.shape[1]
    xyz, core = here(n)
    starts = part_starts(cells)
    lanes = 2 * n * n * n
    none = 2 * n * n
    half = tiles // 2
    halves = (pl.ds(0, half), pl.ds(half, half))

    barrier = pltpu.get_barrier_semaphore()
    count = 0
    for target in partners(n, xyz, core):
        pl.semaphore_signal(barrier, inc=1, device_id=target, device_id_type=MESH)
        count += 1

    loads = []
    for i, (src, dst) in enumerate(((control_hbm, control), (foot_hbm, foot), (obs_hbm, obs))):
        loads.append(pltpu.make_async_copy(src, dst, load_sem.at[i]))
        loads[-1].start()
    load_control, load_foot, load_obs = loads

    lane = lax.broadcasted_iota(I32, (8, lanes), 1)
    wanted = jnp.full((8, lanes), tiles, I32)
    pair = jnp.zeros((8, lanes), I32)
    for b in range(blocks):
        for k in range(touched):
            tile = ids_ref[b, k]
            match = lane == lax.div(tile, tiles)
            wanted = jnp.where(match, lax.rem(tile, tiles), wanted)
            pair = jnp.where(match, b * touched + k, pair)
    pair_v[...] = pair
    mine[...] = wanted
    me = xyz[0] * 2 + core
    row_ids[pl.ds(me, 1)] = wanted[None]
    to_scalar = [pltpu.make_async_copy(pair_v, pair_s, scalar_sem.at[0])]
    to_scalar[0].start()

    corr_h, corr_l = split(corr_ref[...])
    load_control.wait()

    def emit(i, carry):
        t = 2 * i
        both = jnp.concatenate([control[t], control[t + 1]], axis=1)
        both_h, both_l = split(both)
        flux = dot(corr_h, both_h) + (dot(corr_h, both_l) + dot(corr_l, both_h))
        for u in range(2):
            prior = prior_ref[pl.ds(t + u, 1), :]
            base = jnp.concatenate(
                [column(prior[:, members * v : members * (v + 1)]) for v in range(cells // members)], axis=0
            )
            tile = (base + flux[:, members * u : members * (u + 1)]).astype(BF)
            for p in range(3):
                gathered[p][0][t + u] = tile[starts[p] : starts[p] + rows[p]]
        return carry

    lax.fori_loop(0, tiles // 2, emit, 0)

    pl.semaphore_wait(barrier, count)

    sent = []
    row_copies = []
    for dx in range(n):
        for dc in range(2):
            if dx or dc:
                target = device_of(n, moved(n, xyz, 0, dx), lax.rem(core + dc, 2))
                i = dx * 2 + dc
                row_copies.append(remote(mine, row_ids.at[me], id_send.at[i], id_recv.at[i], target))
    sent += row_copies

    one = {}

    def gather(p, k, j, h):
        i = (p * n + (j - k) % n) * 2 + h
        one[p, (j - k) % n, h] = remote(
            gathered[p][j].at[halves[h]], gathered[p][(j - k) % n].at[halves[h]], one_send.at[i], one_recv.at[i],
            device_of(n, moved(n, xyz, ORDERS[p][0], k), core),
        )
        sent.append(one[p, (j - k) % n, h])

    for p in range(3):
        gather(p, 3, 0, 0)
        gather(p, 1, 0, 1)

    for copy in row_copies:
        copy.wait_recv()
    for e in range(2 * n):
        table[xyz[2], xyz[1], e : e + 1, :] = row_ids[e, 0:1, :]
    plane_copies = []
    at = 2 * n
    for dy in range(n):
        for dz in range(n):
            if dy or dz:
                target = device_of(n, moved(n, moved(n, xyz, 1, dy), 2, dz), core)
                i = at + dy * n + dz
                here_ids = table.at[xyz[2], xyz[1]]
                plane_copies.append(remote(here_ids, here_ids, id_send.at[i], id_recv.at[i], target))
    sent += plane_copies

    for p in range(3):
        gather(p, 3, 0, 1)
        gather(p, 1, 0, 0)
    for p in range(3):
        one[p, 1, 0].wait_recv()
        gather(p, 3, 1, 0)
        one[p, 3, 1].wait_recv()
        gather(p, 1, 3, 1)

    for copy in plane_copies:
        copy.wait_recv()
    table_copy = pltpu.make_async_copy(table, table_s, scalar_sem.at[1])
    table_copy.start()
    table_copy.wait()

    two = {}
    for j in (0,) + STEPS:
        for p in range(3):
            if j == 2:
                one[p, 2, 0].wait_recv()
                one[p, 2, 1].wait_recv()
            elif j:
                one[p, j, 1 if j == 1 else 0].wait_recv()
        for kk, k in enumerate(STEPS + (0,)):
            for p, (first, second, third) in enumerate(ORDERS):
                source = lax.rem(xyz[first] + j, n)
                owner = owner_of(n, placed(xyz, first, source), core)
                column_at = moved(n, xyz, second, k)

                def pick(d, carry, p=p, j=j, k=k, kk=kk, third=third, column_at=column_at, owner=owner, source=source,
                         second=second):
                    x, y, z = placed(column_at, third, lax.rem(d, n))
                    tile = table_s[z, y, x * 2 + lax.rem(core + lax.div(d, n), 2), owner]
                    value = gathered[p][j][jnp.clip(tile, 0, tiles - 1)]
                    if k:
                        picked[p][kk, j, d] = value
                    else:
                        middle[p][d, xyz[second], source] = value
                    return carry

                lax.fori_loop(0, 2 * n, pick, 0)
                if k:
                    for other in range(2):
                        i = ((p * n + k) * n + j) * 2 + other
                        span, at_rows = pl.ds(other * n, n), sent_rows(rows, p, other)
                        two[p, k, j, other] = remote(
                            picked[p].at[kk, j, span, at_rows], middle[p].at[span, xyz[second], source, at_rows],
                            two_send.at[i], two_recv.at[i], device_of(n, column_at, core),
                        )
                        sent.append(two[p, k, j, other])

    final = []
    kept = []
    for k in (0,) + STEPS:
        if k:
            for p in range(3):
                for j in range(n):
                    for other in range(2):
                        two[p, k, j, other].wait_recv()
        for ds in STEPS + (0,):
            for other in range(2):
                for p, (first, second, third) in enumerate(ORDERS):
                    source = lax.rem(xyz[second] + n - k, n)
                    mine_at = other * n + xyz[third]
                    at_rows = sent_rows(rows, p, other)
                    goal = moved(n, xyz, third, ds)
                    src = middle[p].at[other * n + goal[third], source, :, at_rows]
                    dst = arrived[p].at[mine_at, source, :, at_rows]
                    if ds or other:
                        i = ((p * n + k) * n + ds) * 2 + other
                        final.append(
                            remote(src, dst, three_send.at[i], three_recv.at[i],
                                   device_of(n, goal, lax.rem(core + other, 2)))
                        )
                    else:
                        kept.append(pltpu.make_async_copy(src, dst, keep_sem.at[p * n + k]))
                        kept[-1].start()
    sent += final

    table_t[...] = table[...].reshape(lanes, lanes).T
    shape = (lanes, lanes)
    coords = []
    for dim in range(2):
        r = lax.broadcasted_iota(I32, shape, dim)
        coords.append(
            ((lax.div(lax.rem(r, 2 * n), 2), lax.rem(lax.div(r, 2 * n), n), lax.div(r, 2 * n * n)), lax.rem(r, 2))
        )
    tile_at = lax.broadcasted_iota(I32, (tiles, lanes), 0)
    last_lane = lax.broadcasted_iota(I32, (tiles, lanes), 1)
    lasts = jnp.full((tiles, lanes), none, I32)
    prev_v[...] = jnp.zeros(prev_v.shape, I32)
    for p, (first, second, third) in enumerate(ORDERS):
        rank = [
            (lax.rem(c[second] + (n - xyz[second]), n) * n + c[third]) * 2 + lax.rem(o + core, 2)
            for c, o in coords
        ]
        in_plane = [c[first] == xyz[first] for c, o in coords]
        earlier = (rank[0] < rank[1]) & in_plane[0]
        for j in range(n):
            owner = owner_of(n, moved(n, xyz, first, j), core)
            across = jnp.broadcast_to(table_t[pl.ds(owner, 1), :], shape)
            down = across.T
            before = jnp.max(jnp.where(earlier & (across == down), rank[0], -1), axis=0, keepdims=True)
            prev_v[p * n + j : p * n + j + 1, :] = jnp.where(before < 0, none, before)
            hit = (across[:tiles] == tile_at) & in_plane[1][:tiles]
            newest = jnp.max(jnp.where(hit, rank[1][:tiles], -1), axis=1, keepdims=True)
            newest = jnp.where(newest < 0, none, newest)
            lasts = jnp.where(last_lane == p * n + j, newest, lasts)
    last_v[...] = lasts
    for i, (src, dst) in enumerate(((prev_v, prev_s), (last_v, last_s))):
        to_scalar.append(pltpu.make_async_copy(src, dst, scalar_sem.at[2 + i]))
        to_scalar[-1].start()
    for p in range(3):
        chain[p][none] = jnp.zeros((rows[p], members), F32)

    load_foot.wait()
    load_obs.wait()
    for copy in to_scalar + kept:
        copy.wait()
    for copy in final:
        copy.wait_recv()
    for copy in sent:
        copy.wait_send()
    freed = 0
    for target in line_partners(n, xyz, core):
        pl.semaphore_signal(free_sem, inc=1, device_id=target, device_id_type=MESH)
        freed += 1

    per = per_block // members

    def model(b, carry):
        feet, flux = [], []
        for k in range(touched):
            tile = lax.div(ids_ref[b, k], tiles)
            oc = lax.rem(tile, 2)
            c = (lax.rem(lax.div(tile, 2), n), lax.div(tile, 2 * n * n), lax.rem(lax.div(tile, 2 * n), n))
            other = lax.rem(oc + core, 2)
            v0, v1, v2 = (
                arrived[p][other * n + c[third], c[second], c[first]]
                for p, (first, second, third) in enumerate(ORDERS)
            )
            shared = jnp.where(other == 0, v0[rows[0] - SHARED :], v1[:SHARED])
            flux += [v0[: rows[0] - SHARED], shared, v1[SHARED:], v2]
            feet.append(foot[b * touched + k])
        modeled = dot(jnp.concatenate(feet, axis=1), jnp.concatenate(flux, axis=0))
        weight = jnp.concatenate([column(weight_ref[pl.ds(b * per + v, 1), :]) for v in range(per)], axis=0)
        wrong = (modeled - obs[pl.ds(pl.multiple_of(b * per_block, per_block), per_block), :]) * weight
        mismatch[b] = wrong.T.astype(BF)
        return carry

    lax.fori_loop(0, blocks, model, 0)

    sent = []
    one_way = {}
    for turn in range(n):

        for other in range(2):

            def make(i, carry, turn=turn, other=other):
                dx, dy = lax.rem(i, n), lax.div(i, n)
                far = (dx, dy, lax.rem(turn + 2 * n - dx - dy, n))
                c = tuple(lax.rem(xyz[a] + far[a], n) for a in range(3))
                pair = jnp.clip(pair_s[0, owner_of(n, c, lax.rem(core + other, 2))], 0, blocks * touched - 1)
                value = dot(mismatch[lax.div(pair, touched)], foot[pair]).astype(BF).T
                for p, (first, second, third) in enumerate(ORDERS):
                    arrived[p][other * n + c[third], lax.rem(far[second] + far[first], n), c[second]] = (
                        value[starts[p] : starts[p] + rows[p]]
                    )
                return carry

            lax.fori_loop(0, n * n, make, 0, unroll=4)
            if turn == 0 and other == 0:
                pl.semaphore_wait(free_sem, freed)
            for ds in STEPS + (0,):
                for p, (first, second, third) in enumerate(ORDERS):
                    goal = moved(n, xyz, third, ds)
                    at_rows = sent_rows(rows, p, other)
                    lies = (turn - ds) % n
                    src = arrived[p].at[other * n + goal[third], lies, :, at_rows]
                    dst = middle[p].at[other * n + xyz[third], lies, :, at_rows]
                    if ds or other:
                        i = ((p * n + turn) * n + ds) * 2 + other
                        copy = remote(src, dst, back_three_send.at[i], back_three_recv.at[i],
                                      device_of(n, goal, lax.rem(core + other, 2)))
                        sent.append(copy)
                    else:
                        copy = pltpu.make_async_copy(src, dst, back_keep_sem.at[p * n + turn])
                        copy.start()
                    one_way.setdefault(p, []).append((copy, bool(ds or other)))

    for p in range(3):
        for copy, far in one_way[p]:
            if far:
                copy.wait_recv()
            else:
                copy.wait()

    two = {}
    for j in BACK + (0,):
        for k in STEPS:
            for p, (first, second, third) in enumerate(ORDERS):
                goal = moved(n, xyz, second, k)
                for other in range(2):
                    span, at_rows = pl.ds(other * n, n), sent_rows(rows, p, other)
                    i = ((p * n + k) * n + j) * 2 + other
                    two[p, k, j, other] = remote(
                        middle[p].at[span, (k + j) % n, goal[second], at_rows],
                        picked[p].at[STEPS.index(n - k), j, span, at_rows],
                        back_two_send.at[i], back_two_recv.at[i], device_of(n, goal, core),
                    )
                    sent.append(two[p, k, j, other])

    one = {}
    relayed = {}

    def give(p, k, j, h, key, src, dst, i):
        copy = remote(
            src, dst, back_one_send.at[i], back_one_recv.at[i],
            device_of(n, moved(n, xyz, ORDERS[p][0], k), core),
        )
        sent.append(copy)
        return copy

    for j in BACK + (0,):
        for p in (1, 2, 0):
            first, second, third = ORDERS[p]
            for k in STEPS:
                for other in range(2):
                    two[p, k, j, other].wait_recv()
            for step in range(n):

                def link(third_at, carry, p=p, j=j, first=first, second=second, third=third, step=step):
                    so = lax.rem(xyz[second] + step, n)
                    c = placed(placed(xyz, second, so), third, third_at)
                    for other in range(2):
                        d = other * n + third_at
                        device = (c[2] * n + c[1]) * (2 * n) + c[0] * 2 + lax.rem(core + other, 2)
                        before = jnp.clip(prev_s[p * n + j, device], 0, none)
                        at = sent_rows(rows, p, other)
                        if step:
                            value = picked[p][STEPS.index(step), j, d, at]
                        else:
                            value = middle[p][d, j, so, at]
                        chain[p][(step * n + third_at) * 2 + other, at] = value.astype(F32) + chain[p][before, at]
                        if at.size < rows[p]:
                            rest = pl.ds(at.size if at.start == 0 else 0, rows[p] - at.size)
                            chain[p][(step * n + third_at) * 2 + other, rest] = chain[p][before, rest]
                    return carry

                lax.fori_loop(0, n, link, 0)

            for h in range(2):
                joins = (j == 1 and h == 0) or (j == 3 and h == 1)
                if joins:
                    relayed[p, h].wait_recv()

                def collect(t, carry, p=p, j=j, h=h, joins=joins):
                    total = chain[p][jnp.clip(last_s[h * half + t, p * n + j], 0, none)]
                    if joins:
                        total = total + relay[p][h, t].astype(F32)
                    if j:
                        gathered[p][j][h * half + t] = total.astype(BF)
                    else:
                        own[p][h * half + t] = total
                    return carry

                lax.fori_loop(0, half, collect, 0)
                if j == 2:
                    k = 1 if h == 0 else 3
                    relayed[p, h] = give(
                        p, k, j, h, "relay", gathered[p][j].at[halves[h]], relay[p].at[h], (p * n + 2) * 2 + h
                    )
                elif j:
                    one[p, j, h] = give(
                        p, j, j, h, "sum", gathered[p][j].at[halves[h]],
                        sums_in[p].at[0 if j == 1 else 1, halves[h]], (p * n + j) * 2 + h,
                    )

    corr_h, corr_l = split(corr_ref[...].T)
    stores = []
    for h in range(2):
        for p in (1, 2, 0):
            for j in (1, 3):
                one[p, j, h].wait_recv()

        def finish(i, carry, h=h):
            t = h * half + 2 * i
            adjoint = []
            for u in range(2):
                v0, v1, v2 = (
                    own[p][t + u] + (sums_in[p][0, t + u].astype(F32) + sums_in[p][1, t + u].astype(F32))
                    for p in range(3)
                )
                shared = v0[rows[0] - SHARED :] + v1[:SHARED]
                adjoint.append(jnp.concatenate([v0[: rows[0] - SHARED], shared, v1[SHARED:], v2], axis=0))
            both_h, both_l = split(jnp.concatenate(adjoint, axis=1))
            spread = dot(corr_h, both_h) + (dot(corr_h, both_l) + dot(corr_l, both_h))
            for u in range(2):
                out[t + u] = control[t + u] + spread[:, members * u : members * (u + 1)]
            return carry

        lax.fori_loop(0, half // 2, finish, 0)
        stores.append(pltpu.make_async_copy(out.at[halves[h]], out_hbm.at[halves[h]], out_sem.at[h]))
        stores[-1].start()

    for copy in sent:
        copy.wait_send()
    for copy in stores:
        copy.wait()


def per_device(n, control, prior_flux, correlation, footprints, obs_values, obs_weights, tile_ids):
    tiles, cells, members = control.shape
    blocks, touched = tile_ids.shape
    per_block = footprints.shape[2]
    owners = 2 * n * n * n
    rows = part_rows(cells)
    foot = footprints.reshape(blocks * touched, per_block, cells)
    vmem, smem, anywhere = (
        pl.BlockSpec(memory_space=pltpu.VMEM),
        pl.BlockSpec(memory_space=pltpu.SMEM),
        pl.BlockSpec(memory_space=pl.ANY),
    )

    def dma(count):
        return pltpu.SemaphoreType.DMA((count,))

    return pl.pallas_call(
        functools.partial(kernel, n, rows),
        name="gradient",
        out_shape=jax.ShapeDtypeStruct(control.shape, F32),
        in_specs=[smem, vmem, vmem, vmem, anywhere, anywhere, anywhere],
        out_specs=anywhere,
        scratch_shapes=(
            [pltpu.VMEM((tiles, r, members), BF) for r in rows for _ in range(4)]
            + [pltpu.VMEM((n - 1, n, 2 * n, r, members), BF) for r in rows]
            + [pltpu.VMEM((2 * n, n, n, r, members), BF) for r in rows]
            + [pltpu.VMEM((2 * n, n, n, r, members), BF) for r in rows]
            + [pltpu.VMEM((2 * n * n + 1, r, members), F32) for r in rows]
            + [pltpu.VMEM((2, tiles, r, members), BF) for r in rows]
            + [pltpu.VMEM((2, tiles // 2, r, members), BF) for r in rows]
            + [pltpu.VMEM((tiles, r, members), F32) for r in rows]
            + [
                pltpu.VMEM((blocks * touched, per_block, cells), BF),
                pltpu.VMEM(control.shape, F32),
                pltpu.VMEM(obs_values.shape, F32),
                pltpu.VMEM(control.shape, F32),
                pltpu.VMEM((blocks, members, per_block), BF),
                pltpu.VMEM((8, owners), I32),
                pltpu.VMEM((2 * n, 8, owners), I32),
                pltpu.VMEM((n, n, 2 * n, owners), I32),
                pltpu.VMEM((owners, owners), I32),
                pltpu.VMEM((8, owners), I32),
                pltpu.VMEM((16, owners), I32),
                pltpu.VMEM((tiles, owners), I32),
                pltpu.SMEM((n, n, 2 * n, owners), I32),
                pltpu.SMEM((8, owners), I32),
                pltpu.SMEM((16, owners), I32),
                pltpu.SMEM((tiles, owners), I32),
                dma(3), dma(2 * n + n * n), dma(2 * n + n * n), dma(4),
                dma(6 * n), dma(6 * n),
                dma(6 * n * n), dma(6 * n * n),
                dma(6 * n * n), dma(6 * n * n), dma(3 * n),
                dma(6 * n * n), dma(6 * n * n), dma(3 * n),
                dma(6 * n * n), dma(6 * n * n),
                dma(6 * n), dma(6 * n),
                dma(2), pltpu.SemaphoreType.REGULAR,
            ]
        ),
        compiler_params=pltpu.CompilerParams(
            collective_id=0, has_side_effects=True, vmem_limit_bytes=VMEM_BYTES
        ),
    )(tile_ids, prior_flux, correlation, obs_weights.reshape(-1, members), control, foot, obs_values)


def solution(mesh):
    n = mesh.shape["emis"] // 2
    return jax.shard_map(
        functools.partial(per_device, n),
        mesh=mesh,
        in_specs=(
            P(("obs", "emis"), None, None),
            P(("obs", "emis"), None),
            P(),
            P(("obs", "emis"), None, None, None),
            P(("obs", "emis"), None),
            P(("obs", "emis")),
            P(("obs", "emis"), None),
        ),
        out_specs=P(("obs", "emis"), None, None),
        check_vma=False,
    )
```

```python
import functools

import jax
import jax.numpy as jnp
from jax import lax
from jax.experimental import pallas as pl
from jax.experimental.pallas import tpu as pltpu
from jax.sharding import PartitionSpec as P

MESH = pl.DeviceIdType.MESH
BF = jnp.bfloat16
F32 = jnp.float32
I32 = jnp.int32
VMEM_BYTES = 60 * 2**20

ORDERS = ((0, 1, 2), (1, 2, 0), (2, 0, 1))


SHARED = 16


def part_starts(cells):
    third = cells // 48 * 16
    return (0, third, cells - third)


def part_rows(cells):
    third = cells // 48 * 16
    return (third + SHARED, third + SHARED, third)


def sent_rows(rows, p, other):
    if p == 0 and other:
        return pl.ds(0, rows[0] - SHARED)
    if p == 1 and not other:
        return pl.ds(SHARED, rows[1] - SHARED)
    return pl.ds(0, rows[p])


STEPS = (1, 3, 2)
BACK = (2, 1, 3)


def here(n):
    o, e = lax.axis_index("obs"), lax.axis_index("emis")
    return (lax.div(e, 2), lax.div(o, n), lax.rem(o, n)), lax.rem(e, 2)


def device_of(n, xyz, core):
    return (xyz[1] * n + xyz[2], xyz[0] * 2 + core)


def owner_of(n, xyz, core):
    return ((xyz[1] * n + xyz[2]) * n + xyz[0]) * 2 + core


def moved(n, xyz, axis, k):
    return tuple(lax.rem(v + k, n) if a == axis else v for a, v in enumerate(xyz))


def placed(xyz, axis, value):
    return tuple(value if a == axis else v for a, v in enumerate(xyz))


def remote(src, dst, send, recv, device):
    copy = pltpu.make_async_remote_copy(
        src_ref=src, dst_ref=dst, send_sem=send, recv_sem=recv, device_id=device, device_id_type=MESH
    )
    copy.start()
    return copy


def line_partners(n, xyz, core):
    for axis in range(3):
        for k in range(1, n):
            for dc in range(2):
                yield device_of(n, moved(n, xyz, axis, k), lax.rem(core + dc, 2))
    yield device_of(n, xyz, 1 - core)


def partners(n, xyz, core):
    yield from line_partners(n, xyz, core)
    for dy in range(1, n):
        for dz in range(1, n):
            yield device_of(n, moved(n, moved(n, xyz, 1, dy), 2, dz), core)


def split(value):
    high = value.astype(BF)
    return high, (value - high.astype(F32)).astype(BF)


def dot(a, b):
    return jnp.dot(a, b, preferred_element_type=F32)


def column(row):
    return jnp.broadcast_to(row, (row.shape[1], row.shape[1])).T


def kernel(
    n, rows, ids_ref, prior_ref, corr_ref, weight_ref, control_hbm, foot_hbm, obs_hbm,
    out_hbm,
    g00, g01, g02, g03, g10, g11, g12, g13, g20, g21, g22, g23,
    s0, s1, s2, b0, b1, b2, a0, a1, a2, h0, h1, h2, r0, r1, r2, m0, m1, m2, o0, o1, o2,
    foot, control, obs, out, weights, mismatch, mine, row_ids, table, table_t, pair_v, prev_v, last_v,
    table_s, pair_s, prev_s, last_s,
    load_sem, id_send, id_recv, scalar_sem, one_send, one_recv, two_send, two_recv, three_send, three_recv, keep_sem,
    back_three_send, back_three_recv, back_keep_sem, back_two_send, back_two_recv, back_one_send, back_one_recv,
    out_sem, free_sem,
):
    gathered = ((g00, g01, g02, g03), (g10, g11, g12, g13), (g20, g21, g22, g23))
    picked, middle, arrived = (s0, s1, s2), (b0, b1, b2), (a0, a1, a2)
    chain, sums_in, relay, own = (h0, h1, h2), (r0, r1, r2), (m0, m1, m2), (o0, o1, o2)
    tiles, cells, members = control.shape
    blocks, touched = ids_ref.shape
    per_block = foot.shape[1]
    xyz, core = here(n)
    starts = part_starts(cells)
    lanes = 2 * n * n * n
    none = 2 * n * n
    half = tiles // 2
    halves = (pl.ds(0, half), pl.ds(half, half))

    barrier = pltpu.get_barrier_semaphore()
    count = 0
    for target in partners(n, xyz, core):
        pl.semaphore_signal(barrier, inc=1, device_id=target, device_id_type=MESH)
        count += 1

    loads = []
    for i, (src, dst) in enumerate(((control_hbm, control), (foot_hbm, foot), (obs_hbm, obs))):
        loads.append(pltpu.make_async_copy(src, dst, load_sem.at[i]))
        loads[-1].start()
    load_control, load_foot, load_obs = loads

    lane = lax.broadcasted_iota(I32, (8, lanes), 1)
    wanted = jnp.full((8, lanes), tiles, I32)
    pair = jnp.zeros((8, lanes), I32)
    for b in range(blocks):
        for k in range(touched):
            tile = ids_ref[b, k]
            match = lane == lax.div(tile, tiles)
            wanted = jnp.where(match, lax.rem(tile, tiles), wanted)
            pair = jnp.where(match, b * touched + k, pair)
    pair_v[...] = pair
    mine[...] = wanted
    me = xyz[0] * 2 + core
    row_ids[pl.ds(me, 1)] = wanted[None]
    to_scalar = [pltpu.make_async_copy(pair_v, pair_s, scalar_sem.at[0])]
    to_scalar[0].start()

    corr_h, corr_l = split(corr_ref[...])
    load_control.wait()

    def emit(i, carry):
        t = 2 * i
        both = jnp.concatenate([control[t], control[t + 1]], axis=1)
        both_h, both_l = split(both)
        flux = dot(corr_h, both_h) + (dot(corr_h, both_l) + dot(corr_l, both_h))
        for u in range(2):
            prior = prior_ref[pl.ds(t + u, 1), :]
            base = jnp.concatenate(
                [column(prior[:, members * v : members * (v + 1)]) for v in range(cells // members)], axis=0
            )
            tile = (base + flux[:, members * u : members * (u + 1)]).astype(BF)
            for p in range(3):
                gathered[p][0][t + u] = tile[starts[p] : starts[p] + rows[p]]
        return carry

    lax.fori_loop(0, tiles // 2, emit, 0)

    pl.semaphore_wait(barrier, count)

    sent = []
    row_copies = []
    for dx in range(n):
        for dc in range(2):
            if dx or dc:
                target = device_of(n, moved(n, xyz, 0, dx), lax.rem(core + dc, 2))
                i = dx * 2 + dc
                row_copies.append(remote(mine, row_ids.at[me], id_send.at[i], id_recv.at[i], target))
    sent += row_copies

    one = {}

    def gather(p, k, j, h):
        i = (p * n + (j - k) % n) * 2 + h
        one[p, (j - k) % n, h] = remote(
            gathered[p][j].at[halves[h]], gathered[p][(j - k) % n].at[halves[h]], one_send.at[i], one_recv.at[i],
            device_of(n, moved(n, xyz, ORDERS[p][0], k), core),
        )
        sent.append(one[p, (j - k) % n, h])

    for p in range(3):
        gather(p, 3, 0, 0)
        gather(p, 1, 0, 1)

    for copy in row_copies:
        copy.wait_recv()
    for e in range(2 * n):
        table[xyz[2], xyz[1], e : e + 1, :] = row_ids[e, 0:1, :]
    plane_copies = []
    at = 2 * n
    for dy in range(n):
        for dz in range(n):
            if dy or dz:
                target = device_of(n, moved(n, moved(n, xyz, 1, dy), 2, dz), core)
                i = at + dy * n + dz
                here_ids = table.at[xyz[2], xyz[1]]
                plane_copies.append(remote(here_ids, here_ids, id_send.at[i], id_recv.at[i], target))
    sent += plane_copies

    for p in range(3):
        gather(p, 3, 0, 1)
        gather(p, 1, 0, 0)
    for p in range(3):
        one[p, 1, 0].wait_recv()
        gather(p, 3, 1, 0)
        one[p, 3, 1].wait_recv()
        gather(p, 1, 3, 1)

    for copy in plane_copies:
        copy.wait_recv()
    table_copy = pltpu.make_async_copy(table, table_s, scalar_sem.at[1])
    table_copy.start()
    table_copy.wait()

    two = {}
    for j in (0,) + STEPS:
        for p in range(3):
            if j == 2:
                one[p, 2, 0].wait_recv()
                one[p, 2, 1].wait_recv()
            elif j:
                one[p, j, 1 if j == 1 else 0].wait_recv()
        for kk, k in enumerate(STEPS + (0,)):
            for p, (first, second, third) in enumerate(ORDERS):
                source = lax.rem(xyz[first] + j, n)
                owner = owner_of(n, placed(xyz, first, source), core)
                column_at = moved(n, xyz, second, k)

                def pick(d, carry, p=p, j=j, k=k, kk=kk, third=third, column_at=column_at, owner=owner, source=source,
                         second=second):
                    x, y, z = placed(column_at, third, lax.rem(d, n))
                    tile = table_s[z, y, x * 2 + lax.rem(core + lax.div(d, n), 2), owner]
                    value = gathered[p][j][jnp.clip(tile, 0, tiles - 1)]
                    if k:
                        picked[p][kk, j, d] = value
                    else:
                        middle[p][d, xyz[second], source] = value
                    return carry

                lax.fori_loop(0, 2 * n, pick, 0)
                if k:
                    for other in range(2):
                        i = ((p * n + k) * n + j) * 2 + other
                        span, at_rows = pl.ds(other * n, n), sent_rows(rows, p, other)
                        two[p, k, j, other] = remote(
                            picked[p].at[kk, j, span, at_rows], middle[p].at[span, xyz[second], source, at_rows],
                            two_send.at[i], two_recv.at[i], device_of(n, column_at, core),
                        )
                        sent.append(two[p, k, j, other])

    final = []
    kept = []
    for k in (0,) + STEPS:
        if k:
            for p in range(3):
                for j in range(n):
                    for other in range(2):
                        two[p, k, j, other].wait_recv()
        for ds in STEPS + (0,):
            for other in range(2):
                for p, (first, second, third) in enumerate(ORDERS):
                    source = lax.rem(xyz[second] + n - k, n)
                    mine_at = other * n + xyz[third]
                    at_rows = sent_rows(rows, p, other)
                    goal = moved(n, xyz, third, ds)
                    src = middle[p].at[other * n + goal[third], source, :, at_rows]
                    dst = arrived[p].at[mine_at, source, :, at_rows]
                    if ds or other:
                        i = ((p * n + k) * n + ds) * 2 + other
                        final.append(
                            remote(src, dst, three_send.at[i], three_recv.at[i],
                                   device_of(n, goal, lax.rem(core + other, 2)))
                        )
                    else:
                        kept.append(pltpu.make_async_copy(src, dst, keep_sem.at[p * n + k]))
                        kept[-1].start()
    sent += final

    table_t[...] = table[...].reshape(lanes, lanes).T
    shape = (lanes, lanes)
    coords = []
    for dim in range(2):
        r = lax.broadcasted_iota(I32, shape, dim)
        coords.append(
            ((lax.div(lax.rem(r, 2 * n), 2), lax.rem(lax.div(r, 2 * n), n), lax.div(r, 2 * n * n)), lax.rem(r, 2))
        )
    tile_at = lax.broadcasted_iota(I32, (tiles, lanes), 0)
    last_lane = lax.broadcasted_iota(I32, (tiles, lanes), 1)
    lasts = jnp.full((tiles, lanes), none, I32)
    prev_v[...] = jnp.zeros(prev_v.shape, I32)
    for p, (first, second, third) in enumerate(ORDERS):
        rank = [
            (lax.rem(c[second] + (n - xyz[second]), n) * n + c[third]) * 2 + lax.rem(o + core, 2)
            for c, o in coords
        ]
        in_plane = [c[first] == xyz[first] for c, o in coords]
        earlier = (rank[0] < rank[1]) & in_plane[0]
        for j in range(n):
            owner = owner_of(n, moved(n, xyz, first, j), core)
            across = jnp.broadcast_to(table_t[pl.ds(owner, 1), :], shape)
            down = across.T
            before = jnp.max(jnp.where(earlier & (across == down), rank[0], -1), axis=0, keepdims=True)
            prev_v[p * n + j : p * n + j + 1, :] = jnp.where(before < 0, none, before)
            hit = (across[:tiles] == tile_at) & in_plane[1][:tiles]
            newest = jnp.max(jnp.where(hit, rank[1][:tiles], -1), axis=1, keepdims=True)
            newest = jnp.where(newest < 0, none, newest)
            lasts = jnp.where(last_lane == p * n + j, newest, lasts)
    last_v[...] = lasts
    for i, (src, dst) in enumerate(((prev_v, prev_s), (last_v, last_s))):
        to_scalar.append(pltpu.make_async_copy(src, dst, scalar_sem.at[2 + i]))
        to_scalar[-1].start()
    for p in range(3):
        chain[p][none] = jnp.zeros((rows[p], members), F32)

    per = per_block // members
    for b in range(blocks):
        for v in range(per):
            weights[b, v * members : (v + 1) * members] = column(weight_ref[b * per + v : b * per + v + 1, :])

    load_foot.wait()
    load_obs.wait()
    for copy in to_scalar + kept:
        copy.wait()
    for copy in final:
        copy.wait_recv()
    for copy in sent:
        copy.wait_send()
    freed = 0
    for target in line_partners(n, xyz, core):
        pl.semaphore_signal(free_sem, inc=1, device_id=target, device_id_type=MESH)
        freed += 1

    def model(b, carry):
        feet, flux = [], []
        for k in range(touched):
            tile = lax.div(ids_ref[b, k], tiles)
            oc = lax.rem(tile, 2)
            c = (lax.rem(lax.div(tile, 2), n), lax.div(tile, 2 * n * n), lax.rem(lax.div(tile, 2 * n), n))
            other = lax.rem(oc + core, 2)
            v0, v1, v2 = (
                arrived[p][other * n + c[third], c[second], c[first]]
                for p, (first, second, third) in enumerate(ORDERS)
            )
            shared = jnp.where(other == 0, v0[rows[0] - SHARED :], v1[:SHARED])
            flux += [v0[: rows[0] - SHARED], shared, v1[SHARED:], v2]
            feet.append(foot[b * touched + k])
        modeled = dot(jnp.concatenate(feet, axis=1), jnp.concatenate(flux, axis=0))
        wrong = (modeled - obs[pl.ds(pl.multiple_of(b * per_block, per_block), per_block), :]) * weights[b]
        mismatch[b] = wrong.T.astype(BF)
        return carry

    lax.fori_loop(0, blocks, model, 0)

    sent = []
    one_way = {}

    def give_back(turn, ds, other):
        for p, (first, second, third) in enumerate(ORDERS):
            goal = moved(n, xyz, third, ds)
            at_rows = sent_rows(rows, p, other)
            lies = (turn - ds) % n
            src = arrived[p].at[other * n + goal[third], lies, :, at_rows]
            dst = middle[p].at[other * n + xyz[third], lies, :, at_rows]
            if ds or other:
                i = ((p * n + turn) * n + ds) * 2 + other
                copy = remote(src, dst, back_three_send.at[i], back_three_recv.at[i],
                              device_of(n, goal, lax.rem(core + other, 2)))
                sent.append(copy)
            else:
                copy = pltpu.make_async_copy(src, dst, back_keep_sem.at[p * n + turn])
                copy.start()
            one_way.setdefault((p, lies), []).append((copy, bool(ds or other)))

    for turn in range(n):

        for other in range(2):

            def make(i, carry, turn=turn, other=other):
                dx, dy = lax.rem(i, n), lax.div(i, n)
                far = (dx, dy, lax.rem(turn + 2 * n - dx - dy, n))
                c = tuple(lax.rem(xyz[a] + far[a], n) for a in range(3))
                pair = jnp.clip(pair_s[0, owner_of(n, c, lax.rem(core + other, 2))], 0, blocks * touched - 1)
                value = dot(mismatch[lax.div(pair, touched)], foot[pair]).astype(BF).T
                for p, (first, second, third) in enumerate(ORDERS):
                    arrived[p][other * n + c[third], lax.rem(far[second] + far[first], n), c[second]] = (
                        value[starts[p] : starts[p] + rows[p]]
                    )
                return carry

            lax.fori_loop(0, n * n, make, 0, unroll=4)
            if turn == 0 and other == 0:
                pl.semaphore_wait(free_sem, freed)
            for ds in STEPS + (0,):
                if turn == 0 or ds == turn:
                    give_back(turn, ds, other)

    for turn in range(1, n):
        for other in range(2):
            for ds in STEPS + (0,):
                if ds != turn:
                    give_back(turn, ds, other)

    def arrive(first_lies):
        for (p, lies), copies in one_way.items():
            if (lies == 0) == first_lies:
                for copy, far in copies:
                    if far:
                        copy.wait_recv()
                    else:
                        copy.wait()

    two = {}

    def pass_on(j, steps):
        for k in steps:
            for p, (first, second, third) in enumerate(ORDERS):
                goal = moved(n, xyz, second, k)
                for other in range(2):
                    span, at_rows = pl.ds(other * n, n), sent_rows(rows, p, other)
                    i = ((p * n + k) * n + j) * 2 + other
                    two[p, k, j, other] = remote(
                        middle[p].at[span, (k + j) % n, goal[second], at_rows],
                        picked[p].at[STEPS.index(n - k), j, span, at_rows],
                        back_two_send.at[i], back_two_recv.at[i], device_of(n, goal, core),
                    )
                    sent.append(two[p, k, j, other])

    arrive(True)
    for j in BACK:
        pass_on(j, (n - j,))
    arrive(False)
    for j in BACK:
        pass_on(j, [k for k in STEPS if k != n - j])

    one = {}
    relayed = {}

    def give(p, k, j, h, key, src, dst, i):
        copy = remote(
            src, dst, back_one_send.at[i], back_one_recv.at[i],
            device_of(n, moved(n, xyz, ORDERS[p][0], k), core),
        )
        sent.append(copy)
        return copy

    for j in BACK + (0,):
        if j == 1:
            pass_on(0, STEPS)
        for p in (1, 2, 0):
            first, second, third = ORDERS[p]
            for k in STEPS:
                for other in range(2):
                    two[p, k, j, other].wait_recv()
            for step in range(n):

                def link(third_at, carry, p=p, j=j, first=first, second=second, third=third, step=step):
                    so = lax.rem(xyz[second] + step, n)
                    c = placed(placed(xyz, second, so), third, third_at)
                    for other in range(2):
                        d = other * n + third_at
                        device = (c[2] * n + c[1]) * (2 * n) + c[0] * 2 + lax.rem(core + other, 2)
                        before = jnp.clip(prev_s[p * n + j, device], 0, none)
                        at = sent_rows(rows, p, other)
                        if step:
                            value = picked[p][STEPS.index(step), j, d, at]
                        else:
                            value = middle[p][d, j, so, at]
                        chain[p][(step * n + third_at) * 2 + other, at] = value.astype(F32) + chain[p][before, at]
                        if at.size < rows[p]:
                            rest = pl.ds(at.size if at.start == 0 else 0, rows[p] - at.size)
                            chain[p][(step * n + third_at) * 2 + other, rest] = chain[p][before, rest]
                    return carry

                lax.fori_loop(0, n, link, 0)

            for h in range(2):
                joins = (j == 1 and h == 0) or (j == 3 and h == 1)
                if joins:
                    relayed[p, h].wait_recv()

                def collect(t, carry, p=p, j=j, h=h, joins=joins):
                    total = chain[p][jnp.clip(last_s[h * half + t, p * n + j], 0, none)]
                    if joins:
                        total = total + relay[p][h, t].astype(F32)
                    if j:
                        gathered[p][j][h * half + t] = total.astype(BF)
                    else:
                        own[p][h * half + t] = total
                    return carry

                lax.fori_loop(0, half, collect, 0)
                if j == 2:
                    k = 1 if h == 0 else 3
                    relayed[p, h] = give(
                        p, k, j, h, "relay", gathered[p][j].at[halves[h]], relay[p].at[h], (p * n + 2) * 2 + h
                    )
                elif j:
                    one[p, j, h] = give(
                        p, j, j, h, "sum", gathered[p][j].at[halves[h]],
                        sums_in[p].at[0 if j == 1 else 1, halves[h]], (p * n + j) * 2 + h,
                    )

    corr_h, corr_l = split(corr_ref[...].T)
    stores = []
    for h in range(2):
        for p in (1, 2, 0):
            for j in (1, 3):
                one[p, j, h].wait_recv()

        def finish(i, carry, h=h):
            t = h * half + 2 * i
            adjoint = []
            for u in range(2):
                v0, v1, v2 = (
                    own[p][t + u] + (sums_in[p][0, t + u].astype(F32) + sums_in[p][1, t + u].astype(F32))
                    for p in range(3)
                )
                shared = v0[rows[0] - SHARED :] + v1[:SHARED]
                adjoint.append(jnp.concatenate([v0[: rows[0] - SHARED], shared, v1[SHARED:], v2], axis=0))
            both_h, both_l = split(jnp.concatenate(adjoint, axis=1))
            spread = dot(corr_h, both_h) + (dot(corr_h, both_l) + dot(corr_l, both_h))
            for u in range(2):
                out[t + u] = control[t + u] + spread[:, members * u : members * (u + 1)]
            return carry

        lax.fori_loop(0, half // 2, finish, 0)
        stores.append(pltpu.make_async_copy(out.at[halves[h]], out_hbm.at[halves[h]], out_sem.at[h]))
        stores[-1].start()

    for copy in sent:
        copy.wait_send()
    for copy in stores:
        copy.wait()


def per_device(n, control, prior_flux, correlation, footprints, obs_values, obs_weights, tile_ids):
    tiles, cells, members = control.shape
    blocks, touched = tile_ids.shape
    per_block = footprints.shape[2]
    owners = 2 * n * n * n
    rows = part_rows(cells)
    foot = footprints.reshape(blocks * touched, per_block, cells)
    vmem, smem, anywhere = (
        pl.BlockSpec(memory_space=pltpu.VMEM),
        pl.BlockSpec(memory_space=pltpu.SMEM),
        pl.BlockSpec(memory_space=pl.ANY),
    )

    def dma(count):
        return pltpu.SemaphoreType.DMA((count,))

    return pl.pallas_call(
        functools.partial(kernel, n, rows),
        name="gradient",
        out_shape=jax.ShapeDtypeStruct(control.shape, F32),
        in_specs=[smem, vmem, vmem, vmem, anywhere, anywhere, anywhere],
        out_specs=anywhere,
        scratch_shapes=(
            [pltpu.VMEM((tiles, r, members), BF) for r in rows for _ in range(4)]
            + [pltpu.VMEM((n - 1, n, 2 * n, r, members), BF) for r in rows]
            + [pltpu.VMEM((2 * n, n, n, r, members), BF) for r in rows]
            + [pltpu.VMEM((2 * n, n, n, r, members), BF) for r in rows]
            + [pltpu.VMEM((2 * n * n + 1, r, members), F32) for r in rows]
            + [pltpu.VMEM((2, tiles, r, members), BF) for r in rows]
            + [pltpu.VMEM((2, tiles // 2, r, members), BF) for r in rows]
            + [pltpu.VMEM((tiles, r, members), F32) for r in rows]
            + [
                pltpu.VMEM((blocks * touched, per_block, cells), BF),
                pltpu.VMEM(control.shape, F32),
                pltpu.VMEM(obs_values.shape, F32),
                pltpu.VMEM(control.shape, F32),
                pltpu.VMEM((blocks, per_block, members), F32),
                pltpu.VMEM((blocks, members, per_block), BF),
                pltpu.VMEM((8, owners), I32),
                pltpu.VMEM((2 * n, 8, owners), I32),
                pltpu.VMEM((n, n, 2 * n, owners), I32),
                pltpu.VMEM((owners, owners), I32),
                pltpu.VMEM((8, owners), I32),
                pltpu.VMEM((16, owners), I32),
                pltpu.VMEM((tiles, owners), I32),
                pltpu.SMEM((n, n, 2 * n, owners), I32),
                pltpu.SMEM((8, owners), I32),
                pltpu.SMEM((16, owners), I32),
                pltpu.SMEM((tiles, owners), I32),
                dma(3), dma(2 * n + n * n), dma(2 * n + n * n), dma(4),
                dma(6 * n), dma(6 * n),
                dma(6 * n * n), dma(6 * n * n),
                dma(6 * n * n), dma(6 * n * n), dma(3 * n),
                dma(6 * n * n), dma(6 * n * n), dma(3 * n),
                dma(6 * n * n), dma(6 * n * n),
                dma(6 * n), dma(6 * n),
                dma(2), pltpu.SemaphoreType.REGULAR,
            ]
        ),
        compiler_params=pltpu.CompilerParams(
            collective_id=0, has_side_effects=True, vmem_limit_bytes=VMEM_BYTES
        ),
    )(tile_ids, prior_flux, correlation, obs_weights.reshape(-1, members), control, foot, obs_values)


def solution(mesh):
    n = mesh.shape["emis"] // 2
    return jax.shard_map(
        functools.partial(per_device, n),
        mesh=mesh,
        in_specs=(
            P(("obs", "emis"), None, None),
            P(("obs", "emis"), None),
            P(),
            P(("obs", "emis"), None, None, None),
            P(("obs", "emis"), None),
            P(("obs", "emis")),
            P(("obs", "emis"), None),
        ),
        out_specs=P(("obs", "emis"), None, None),
        check_vma=False,
    )
```

```python
import functools

import jax
import jax.numpy as jnp
from jax import lax
from jax.experimental import pallas as pl
from jax.experimental.pallas import tpu as pltpu
from jax.sharding import PartitionSpec as P

MESH = pl.DeviceIdType.MESH
BF = jnp.bfloat16
F32 = jnp.float32
I32 = jnp.int32
VMEM_BYTES = 60 * 2**20

ORDERS = ((0, 1, 2), (1, 2, 0), (2, 0, 1))


SHARED = 16


def part_starts(cells):
    third = cells // 48 * 16
    return (0, third, cells - third)


def part_rows(cells):
    third = cells // 48 * 16
    return (third + SHARED, third + SHARED, third)


def sent_rows(rows, p, other):
    if p == 0 and other:
        return pl.ds(0, rows[0] - SHARED)
    if p == 1 and not other:
        return pl.ds(SHARED, rows[1] - SHARED)
    return pl.ds(0, rows[p])


STEPS = (1, 3, 2)
BACK = (2, 1, 3)


def here(n):
    o, e = lax.axis_index("obs"), lax.axis_index("emis")
    return (lax.div(e, 2), lax.div(o, n), lax.rem(o, n)), lax.rem(e, 2)


def device_of(n, xyz, core):
    return (xyz[1] * n + xyz[2], xyz[0] * 2 + core)


def owner_of(n, xyz, core):
    return ((xyz[1] * n + xyz[2]) * n + xyz[0]) * 2 + core


def moved(n, xyz, axis, k):
    return tuple(lax.rem(v + k, n) if a == axis else v for a, v in enumerate(xyz))


def placed(xyz, axis, value):
    return tuple(value if a == axis else v for a, v in enumerate(xyz))


def remote(src, dst, send, recv, device):
    copy = pltpu.make_async_remote_copy(
        src_ref=src, dst_ref=dst, send_sem=send, recv_sem=recv, device_id=device, device_id_type=MESH
    )
    copy.start()
    return copy


def line_partners(n, xyz, core):
    for axis in range(3):
        for k in range(1, n):
            for dc in range(2):
                yield device_of(n, moved(n, xyz, axis, k), lax.rem(core + dc, 2))
    yield device_of(n, xyz, 1 - core)


def partners(n, xyz, core):
    yield from line_partners(n, xyz, core)
    for dy in range(1, n):
        for dz in range(1, n):
            yield device_of(n, moved(n, moved(n, xyz, 1, dy), 2, dz), core)


def split(value):
    high = value.astype(BF)
    return high, (value - high.astype(F32)).astype(BF)


def dot(a, b):
    return jnp.dot(a, b, preferred_element_type=F32)


def column(row):
    return jnp.broadcast_to(row, (row.shape[1], row.shape[1])).T


def kernel(
    n, rows, ids_ref, prior_ref, corr_ref, weight_ref, control_hbm, foot_hbm, obs_hbm,
    out_hbm,
    g00, g01, g02, g03, g10, g11, g12, g13, g20, g21, g22, g23,
    s0, s1, s2, b0, b1, b2, a0, a1, a2, h0, h1, h2, r0, r1, r2, m0, m1, m2, o0, o1, o2,
    foot, control, obs, out, weights, mismatch, mine, row_ids, table, table_t, pair_v, prev_v, last_v,
    table_s, pair_s, prev_s, last_s,
    load_sem, id_send, id_recv, scalar_sem, one_send, one_recv, two_send, two_recv, three_send, three_recv, keep_sem,
    back_three_send, back_three_recv, back_keep_sem, back_two_send, back_two_recv, back_one_send, back_one_recv,
    out_sem, free_sem,
):
    gathered = ((g00, g01, g02, g03), (g10, g11, g12, g13), (g20, g21, g22, g23))
    picked, middle, arrived = (s0, s1, s2), (b0, b1, b2), (a0, a1, a2)
    chain, sums_in, relay, own = (h0, h1, h2), (r0, r1, r2), (m0, m1, m2), (o0, o1, o2)
    tiles, cells, members = control.shape
    blocks, touched = ids_ref.shape
    per_block = foot.shape[1]
    xyz, core = here(n)
    starts = part_starts(cells)
    lanes = 2 * n * n * n
    none = 2 * n * n
    half = tiles // 2
    halves = (pl.ds(0, half), pl.ds(half, half))

    barrier = pltpu.get_barrier_semaphore()
    count = 0
    for target in partners(n, xyz, core):
        pl.semaphore_signal(barrier, inc=1, device_id=target, device_id_type=MESH)
        count += 1

    loads = []
    for i, (src, dst) in enumerate(((control_hbm, control), (foot_hbm, foot), (obs_hbm, obs))):
        loads.append(pltpu.make_async_copy(src, dst, load_sem.at[i]))
        loads[-1].start()
    load_control, load_foot, load_obs = loads

    lane = lax.broadcasted_iota(I32, (8, lanes), 1)
    wanted = jnp.full((8, lanes), tiles, I32)
    pair = jnp.zeros((8, lanes), I32)
    for b in range(blocks):
        for k in range(touched):
            tile = ids_ref[b, k]
            match = lane == lax.div(tile, tiles)
            wanted = jnp.where(match, lax.rem(tile, tiles), wanted)
            pair = jnp.where(match, b * touched + k, pair)
    pair_v[...] = pair
    mine[...] = wanted
    me = xyz[0] * 2 + core
    row_ids[pl.ds(me, 1)] = wanted[None]
    to_scalar = [pltpu.make_async_copy(pair_v, pair_s, scalar_sem.at[0])]
    to_scalar[0].start()

    corr_h, corr_l = split(corr_ref[...])
    load_control.wait()

    def emit(i, carry):
        t = 2 * i
        both = jnp.concatenate([control[t], control[t + 1]], axis=1)
        both_h, both_l = split(both)
        flux = dot(corr_h, both_h) + (dot(corr_h, both_l) + dot(corr_l, both_h))
        for u in range(2):
            prior = prior_ref[pl.ds(t + u, 1), :]
            base = jnp.concatenate(
                [column(prior[:, members * v : members * (v + 1)]) for v in range(cells // members)], axis=0
            )
            tile = (base + flux[:, members * u : members * (u + 1)]).astype(BF)
            for p in range(3):
                gathered[p][0][t + u] = tile[starts[p] : starts[p] + rows[p]]
        return carry

    lax.fori_loop(0, tiles // 2, emit, 0)

    pl.semaphore_wait(barrier, count)

    sent = []
    row_copies = []
    for dx in range(n):
        for dc in range(2):
            if dx or dc:
                target = device_of(n, moved(n, xyz, 0, dx), lax.rem(core + dc, 2))
                i = dx * 2 + dc
                row_copies.append(remote(mine, row_ids.at[me], id_send.at[i], id_recv.at[i], target))
    sent += row_copies

    one = {}

    def gather(p, k, j, h):
        i = (p * n + (j - k) % n) * 2 + h
        one[p, (j - k) % n, h] = remote(
            gathered[p][j].at[halves[h]], gathered[p][(j - k) % n].at[halves[h]], one_send.at[i], one_recv.at[i],
            device_of(n, moved(n, xyz, ORDERS[p][0], k), core),
        )
        sent.append(one[p, (j - k) % n, h])

    for p in range(3):
        gather(p, 3, 0, 0)
        gather(p, 1, 0, 1)

    for copy in row_copies:
        copy.wait_recv()
    for e in range(2 * n):
        table[xyz[2], xyz[1], e : e + 1, :] = row_ids[e, 0:1, :]
    plane_copies = []
    at = 2 * n
    for dy in range(n):
        for dz in range(n):
            if dy or dz:
                target = device_of(n, moved(n, moved(n, xyz, 1, dy), 2, dz), core)
                i = at + dy * n + dz
                here_ids = table.at[xyz[2], xyz[1]]
                plane_copies.append(remote(here_ids, here_ids, id_send.at[i], id_recv.at[i], target))
    sent += plane_copies

    for p in range(3):
        gather(p, 3, 0, 1)
        gather(p, 1, 0, 0)
    for p in range(3):
        one[p, 1, 0].wait_recv()
        gather(p, 3, 1, 0)
        one[p, 3, 1].wait_recv()
        gather(p, 1, 3, 1)

    for copy in plane_copies:
        copy.wait_recv()
    table_copy = pltpu.make_async_copy(table, table_s, scalar_sem.at[1])
    table_copy.start()
    table_copy.wait()

    two = {}
    for j in (0,) + STEPS:
        for p in range(3):
            if j == 2:
                one[p, 2, 0].wait_recv()
                one[p, 2, 1].wait_recv()
            elif j:
                one[p, j, 1 if j == 1 else 0].wait_recv()
        for kk, k in enumerate(STEPS + (0,)):
            for p, (first, second, third) in enumerate(ORDERS):
                source = lax.rem(xyz[first] + j, n)
                owner = owner_of(n, placed(xyz, first, source), core)
                column_at = moved(n, xyz, second, k)

                def pick(d, carry, p=p, j=j, k=k, kk=kk, third=third, column_at=column_at, owner=owner, source=source,
                         second=second):
                    x, y, z = placed(column_at, third, lax.rem(d, n))
                    tile = table_s[z, y, x * 2 + lax.rem(core + lax.div(d, n), 2), owner]
                    value = gathered[p][j][jnp.clip(tile, 0, tiles - 1)]
                    if k:
                        picked[p][kk, j, d] = value
                    else:
                        middle[p][d, xyz[second], source] = value
                    return carry

                lax.fori_loop(0, 2 * n, pick, 0)
                if k:
                    for other in range(2):
                        i = ((p * n + k) * n + j) * 2 + other
                        span, at_rows = pl.ds(other * n, n), sent_rows(rows, p, other)
                        two[p, k, j, other] = remote(
                            picked[p].at[kk, j, span, at_rows], middle[p].at[span, xyz[second], source, at_rows],
                            two_send.at[i], two_recv.at[i], device_of(n, column_at, core),
                        )
                        sent.append(two[p, k, j, other])

    final = []
    kept = []
    for k in (0,) + STEPS:
        if k:
            for p in range(3):
                for j in range(n):
                    for other in range(2):
                        two[p, k, j, other].wait_recv()
        for ds in STEPS + (0,):
            for other in range(2):
                for p, (first, second, third) in enumerate(ORDERS):
                    source = lax.rem(xyz[second] + n - k, n)
                    mine_at = other * n + xyz[third]
                    at_rows = sent_rows(rows, p, other)
                    goal = moved(n, xyz, third, ds)
                    src = middle[p].at[other * n + goal[third], source, :, at_rows]
                    dst = arrived[p].at[mine_at, source, :, at_rows]
                    if ds or other:
                        i = ((p * n + k) * n + ds) * 2 + other
                        final.append(
                            remote(src, dst, three_send.at[i], three_recv.at[i],
                                   device_of(n, goal, lax.rem(core + other, 2)))
                        )
                    else:
                        kept.append(pltpu.make_async_copy(src, dst, keep_sem.at[p * n + k]))
                        kept[-1].start()
    table_t[...] = table[...].reshape(lanes, lanes).T
    shape = (lanes, lanes)
    coords = []
    for dim in range(2):
        r = lax.broadcasted_iota(I32, shape, dim)
        coords.append(
            ((lax.div(lax.rem(r, 2 * n), 2), lax.rem(lax.div(r, 2 * n), n), lax.div(r, 2 * n * n)), lax.rem(r, 2))
        )
    tile_at = lax.broadcasted_iota(I32, (tiles, lanes), 0)
    last_lane = lax.broadcasted_iota(I32, (tiles, lanes), 1)
    lasts = jnp.full((tiles, lanes), none, I32)
    prev_v[...] = jnp.zeros(prev_v.shape, I32)
    for p, (first, second, third) in enumerate(ORDERS):
        rank = [
            (lax.rem(c[second] + (n - xyz[second]), n) * n + c[third]) * 2 + lax.rem(o + core, 2)
            for c, o in coords
        ]
        in_plane = [c[first] == xyz[first] for c, o in coords]
        earlier = (rank[0] < rank[1]) & in_plane[0]
        for j in range(n):
            owner = owner_of(n, moved(n, xyz, first, j), core)
            across = jnp.broadcast_to(table_t[pl.ds(owner, 1), :], shape)
            down = across.T
            before = jnp.max(jnp.where(earlier & (across == down), rank[0], -1), axis=0, keepdims=True)
            prev_v[p * n + j : p * n + j + 1, :] = jnp.where(before < 0, none, before)
            hit = (across[:tiles] == tile_at) & in_plane[1][:tiles]
            newest = jnp.max(jnp.where(hit, rank[1][:tiles], -1), axis=1, keepdims=True)
            newest = jnp.where(newest < 0, none, newest)
            lasts = jnp.where(last_lane == p * n + j, newest, lasts)
    last_v[...] = lasts
    for i, (src, dst) in enumerate(((prev_v, prev_s), (last_v, last_s))):
        to_scalar.append(pltpu.make_async_copy(src, dst, scalar_sem.at[2 + i]))
        to_scalar[-1].start()
    for p in range(3):
        chain[p][none] = jnp.zeros((rows[p], members), F32)

    per = per_block // members
    for b in range(blocks):
        for v in range(per):
            weights[b, v * members : (v + 1) * members] = column(weight_ref[b * per + v : b * per + v + 1, :])

    load_foot.wait()
    load_obs.wait()
    for copy in to_scalar + kept:
        copy.wait()
    for copy in sent:
        copy.wait_send()
    per_step = len(final) // n
    for k in range(n):
        for copy in final[k * per_step : (k + 1) * per_step]:
            copy.wait_recv()
        for copy in final[k * per_step : (k + 1) * per_step]:
            copy.wait_send()
    freed = 0
    for target in line_partners(n, xyz, core):
        pl.semaphore_signal(free_sem, inc=1, device_id=target, device_id_type=MESH)
        freed += 1

    def model(b, carry):
        feet, flux = [], []
        for k in range(touched):
            tile = lax.div(ids_ref[b, k], tiles)
            oc = lax.rem(tile, 2)
            c = (lax.rem(lax.div(tile, 2), n), lax.div(tile, 2 * n * n), lax.rem(lax.div(tile, 2 * n), n))
            other = lax.rem(oc + core, 2)
            v0, v1, v2 = (
                arrived[p][other * n + c[third], c[second], c[first]]
                for p, (first, second, third) in enumerate(ORDERS)
            )
            shared = jnp.where(other == 0, v0[rows[0] - SHARED :], v1[:SHARED])
            flux += [v0[: rows[0] - SHARED], shared, v1[SHARED:], v2]
            feet.append(foot[b * touched + k])
        modeled = dot(jnp.concatenate(feet, axis=1), jnp.concatenate(flux, axis=0))
        wrong = (modeled - obs[pl.ds(pl.multiple_of(b * per_block, per_block), per_block), :]) * weights[b]
        mismatch[b] = wrong.T.astype(BF)
        return carry

    lax.fori_loop(0, blocks, model, 0, unroll=2)

    sent = []
    one_way = {}

    def give_back(turn, ds, other):
        for p, (first, second, third) in enumerate(ORDERS):
            goal = moved(n, xyz, third, ds)
            at_rows = sent_rows(rows, p, other)
            lies = (turn - ds) % n
            src = arrived[p].at[other * n + goal[third], lies, :, at_rows]
            dst = middle[p].at[other * n + xyz[third], lies, :, at_rows]
            if ds or other:
                i = ((p * n + turn) * n + ds) * 2 + other
                copy = remote(src, dst, back_three_send.at[i], back_three_recv.at[i],
                              device_of(n, goal, lax.rem(core + other, 2)))
                sent.append(copy)
            else:
                copy = pltpu.make_async_copy(src, dst, back_keep_sem.at[p * n + turn])
                copy.start()
            one_way.setdefault((p, lies), []).append((copy, bool(ds or other)))

    for turn in range(n):

        for other in range(2):

            def make(i, carry, turn=turn, other=other):
                dx, dy = lax.rem(i, n), lax.div(i, n)
                far = (dx, dy, lax.rem(turn + 2 * n - dx - dy, n))
                c = tuple(lax.rem(xyz[a] + far[a], n) for a in range(3))
                pair = jnp.clip(pair_s[0, owner_of(n, c, lax.rem(core + other, 2))], 0, blocks * touched - 1)
                value = dot(mismatch[lax.div(pair, touched)], foot[pair]).astype(BF).T
                for p, (first, second, third) in enumerate(ORDERS):
                    arrived[p][other * n + c[third], lax.rem(far[second] + far[first], n), c[second]] = (
                        value[starts[p] : starts[p] + rows[p]]
                    )
                return carry

            lax.fori_loop(0, n * n, make, 0, unroll=8)
            if turn == 0 and other == 0:
                pl.semaphore_wait(free_sem, freed)
            for ds in STEPS + (0,):
                if turn == 0 or ds == turn:
                    give_back(turn, ds, other)

    for turn in range(1, n):
        for other in range(2):
            for ds in STEPS + (0,):
                if ds != turn:
                    give_back(turn, ds, other)

    def arrive(first_lies):
        for (p, lies), copies in one_way.items():
            if (lies == 0) == first_lies:
                for copy, far in copies:
                    if far:
                        copy.wait_recv()
                    else:
                        copy.wait()

    two = {}

    def pass_on(j, steps):
        for k in steps:
            for p, (first, second, third) in enumerate(ORDERS):
                goal = moved(n, xyz, second, k)
                for other in range(2):
                    span, at_rows = pl.ds(other * n, n), sent_rows(rows, p, other)
                    i = ((p * n + k) * n + j) * 2 + other
                    two[p, k, j, other] = remote(
                        middle[p].at[span, (k + j) % n, goal[second], at_rows],
                        picked[p].at[STEPS.index(n - k), j, span, at_rows],
                        back_two_send.at[i], back_two_recv.at[i], device_of(n, goal, core),
                    )
                    sent.append(two[p, k, j, other])

    arrive(True)
    for j in BACK:
        pass_on(j, (n - j,))
    arrive(False)
    for j in BACK:
        pass_on(j, [k for k in STEPS if k != n - j])

    one = {}
    relayed = {}

    def give(p, k, j, h, key, src, dst, i):
        copy = remote(
            src, dst, back_one_send.at[i], back_one_recv.at[i],
            device_of(n, moved(n, xyz, ORDERS[p][0], k), core),
        )
        sent.append(copy)
        return copy

    for j in BACK + (0,):
        if j == 1:
            pass_on(0, STEPS)
        for p in (1, 2, 0):
            first, second, third = ORDERS[p]
            for k in STEPS:
                for other in range(2):
                    two[p, k, j, other].wait_recv()
            for step in range(n):

                def link(third_at, carry, p=p, j=j, first=first, second=second, third=third, step=step):
                    so = lax.rem(xyz[second] + step, n)
                    c = placed(placed(xyz, second, so), third, third_at)
                    for other in range(2):
                        d = other * n + third_at
                        device = (c[2] * n + c[1]) * (2 * n) + c[0] * 2 + lax.rem(core + other, 2)
                        before = jnp.clip(prev_s[p * n + j, device], 0, none)
                        at = sent_rows(rows, p, other)
                        if step:
                            value = picked[p][STEPS.index(step), j, d, at]
                        else:
                            value = middle[p][d, j, so, at]
                        chain[p][(step * n + third_at) * 2 + other, at] = value.astype(F32) + chain[p][before, at]
                        if at.size < rows[p]:
                            rest = pl.ds(at.size if at.start == 0 else 0, rows[p] - at.size)
                            chain[p][(step * n + third_at) * 2 + other, rest] = chain[p][before, rest]
                    return carry

                lax.fori_loop(0, n, link, 0)

            for h in range(2):
                joins = (j == 1 and h == 0) or (j == 3 and h == 1)
                if joins:
                    relayed[p, h].wait_recv()

                def collect(t, carry, p=p, j=j, h=h, joins=joins):
                    total = chain[p][jnp.clip(last_s[h * half + t, p * n + j], 0, none)]
                    if joins:
                        total = total + relay[p][h, t].astype(F32)
                    if j:
                        gathered[p][j][h * half + t] = total.astype(BF)
                    else:
                        own[p][h * half + t] = total
                    return carry

                lax.fori_loop(0, half, collect, 0)
                if j == 2:
                    k = 1 if h == 0 else 3
                    relayed[p, h] = give(
                        p, k, j, h, "relay", gathered[p][j].at[halves[h]], relay[p].at[h], (p * n + 2) * 2 + h
                    )
                elif j:
                    one[p, j, h] = give(
                        p, j, j, h, "sum", gathered[p][j].at[halves[h]],
                        sums_in[p].at[0 if j == 1 else 1, halves[h]], (p * n + j) * 2 + h,
                    )

    corr_h, corr_l = split(corr_ref[...].T)
    late = list(one.values())
    for copy in sent:
        if all(copy is not other for other in late):
            copy.wait_send()
    stores = []
    for h in range(2):
        for p in (1, 2, 0):
            for j in (1, 3):
                one[p, j, h].wait_recv()

        def finish(i, carry, h=h):
            t = h * half + 2 * i
            adjoint = []
            for u in range(2):
                v0, v1, v2 = (
                    own[p][t + u] + (sums_in[p][0, t + u].astype(F32) + sums_in[p][1, t + u].astype(F32))
                    for p in range(3)
                )
                shared = v0[rows[0] - SHARED :] + v1[:SHARED]
                adjoint.append(jnp.concatenate([v0[: rows[0] - SHARED], shared, v1[SHARED:], v2], axis=0))
            both_h, both_l = split(jnp.concatenate(adjoint, axis=1))
            spread = dot(corr_h, both_h) + (dot(corr_h, both_l) + dot(corr_l, both_h))
            for u in range(2):
                out[t + u] = control[t + u] + spread[:, members * u : members * (u + 1)]
            return carry

        lax.fori_loop(0, half // 2, finish, 0)
        stores.append(pltpu.make_async_copy(out.at[halves[h]], out_hbm.at[halves[h]], out_sem.at[h]))
        stores[-1].start()

    for copy in late:
        copy.wait_send()
    for copy in stores:
        copy.wait()


def per_device(n, control, prior_flux, correlation, footprints, obs_values, obs_weights, tile_ids):
    tiles, cells, members = control.shape
    blocks, touched = tile_ids.shape
    per_block = footprints.shape[2]
    owners = 2 * n * n * n
    rows = part_rows(cells)
    foot = footprints.reshape(blocks * touched, per_block, cells)
    vmem, smem, anywhere = (
        pl.BlockSpec(memory_space=pltpu.VMEM),
        pl.BlockSpec(memory_space=pltpu.SMEM),
        pl.BlockSpec(memory_space=pl.ANY),
    )

    def dma(count):
        return pltpu.SemaphoreType.DMA((count,))

    return pl.pallas_call(
        functools.partial(kernel, n, rows),
        name="gradient",
        out_shape=jax.ShapeDtypeStruct(control.shape, F32),
        in_specs=[smem, vmem, vmem, vmem, anywhere, anywhere, anywhere],
        out_specs=anywhere,
        scratch_shapes=(
            [pltpu.VMEM((tiles, r, members), BF) for r in rows for _ in range(4)]
            + [pltpu.VMEM((n - 1, n, 2 * n, r, members), BF) for r in rows]
            + [pltpu.VMEM((2 * n, n, n, r, members), BF) for r in rows]
            + [pltpu.VMEM((2 * n, n, n, r, members), BF) for r in rows]
            + [pltpu.VMEM((2 * n * n + 1, r, members), F32) for r in rows]
            + [pltpu.VMEM((2, tiles, r, members), BF) for r in rows]
            + [pltpu.VMEM((2, tiles // 2, r, members), BF) for r in rows]
            + [pltpu.VMEM((tiles, r, members), F32) for r in rows]
            + [
                pltpu.VMEM((blocks * touched, per_block, cells), BF),
                pltpu.VMEM(control.shape, F32),
                pltpu.VMEM(obs_values.shape, F32),
                pltpu.VMEM(control.shape, F32),
                pltpu.VMEM((blocks, per_block, members), F32),
                pltpu.VMEM((blocks, members, per_block), BF),
                pltpu.VMEM((8, owners), I32),
                pltpu.VMEM((2 * n, 8, owners), I32),
                pltpu.VMEM((n, n, 2 * n, owners), I32),
                pltpu.VMEM((owners, owners), I32),
                pltpu.VMEM((8, owners), I32),
                pltpu.VMEM((16, owners), I32),
                pltpu.VMEM((tiles, owners), I32),
                pltpu.SMEM((n, n, 2 * n, owners), I32),
                pltpu.SMEM((8, owners), I32),
                pltpu.SMEM((16, owners), I32),
                pltpu.SMEM((tiles, owners), I32),
                dma(3), dma(2 * n + n * n), dma(2 * n + n * n), dma(4),
                dma(6 * n), dma(6 * n),
                dma(6 * n * n), dma(6 * n * n),
                dma(6 * n * n), dma(6 * n * n), dma(3 * n),
                dma(6 * n * n), dma(6 * n * n), dma(3 * n),
                dma(6 * n * n), dma(6 * n * n),
                dma(6 * n), dma(6 * n),
                dma(2), pltpu.SemaphoreType.REGULAR,
            ]
        ),
        compiler_params=pltpu.CompilerParams(
            collective_id=0, has_side_effects=True, vmem_limit_bytes=VMEM_BYTES
        ),
    )(tile_ids, prior_flux, correlation, obs_weights.reshape(-1, members), control, foot, obs_values)


def solution(mesh):
    n = mesh.shape["emis"] // 2
    return jax.shard_map(
        functools.partial(per_device, n),
        mesh=mesh,
        in_specs=(
            P(("obs", "emis"), None, None),
            P(("obs", "emis"), None),
            P(),
            P(("obs", "emis"), None, None, None),
            P(("obs", "emis"), None),
            P(("obs", "emis")),
            P(("obs", "emis"), None),
        ),
        out_specs=P(("obs", "emis"), None, None),
        check_vma=False,
    )
```

```python
import functools

import jax
import jax.numpy as jnp
from jax import lax
from jax.experimental import pallas as pl
from jax.experimental.pallas import tpu as pltpu
from jax.sharding import PartitionSpec as P

MESH = pl.DeviceIdType.MESH
BF = jnp.bfloat16
F32 = jnp.float32
I32 = jnp.int32
VMEM_BYTES = 60 * 2**20

ORDERS = ((0, 1, 2), (1, 2, 0), (2, 0, 1))


SHARED = 16


def part_starts(cells):
    third = cells // 48 * 16
    return (0, third, cells - third)


def part_rows(cells):
    third = cells // 48 * 16
    return (third + SHARED, third + SHARED, third)


def sent_rows(rows, p, other):
    if p == 0 and other:
        return pl.ds(0, rows[0] - SHARED)
    if p == 1 and not other:
        return pl.ds(SHARED, rows[1] - SHARED)
    return pl.ds(0, rows[p])


STEPS = (1, 3, 2)
BACK = (2, 1, 3)


def here(n):
    o, e = lax.axis_index("obs"), lax.axis_index("emis")
    return (lax.div(e, 2), lax.div(o, n), lax.rem(o, n)), lax.rem(e, 2)


def device_of(n, xyz, core):
    return (xyz[1] * n + xyz[2], xyz[0] * 2 + core)


def owner_of(n, xyz, core):
    return ((xyz[1] * n + xyz[2]) * n + xyz[0]) * 2 + core


def moved(n, xyz, axis, k):
    return tuple(lax.rem(v + k, n) if a == axis else v for a, v in enumerate(xyz))


def placed(xyz, axis, value):
    return tuple(value if a == axis else v for a, v in enumerate(xyz))


def remote(src, dst, send, recv, device):
    copy = pltpu.make_async_remote_copy(
        src_ref=src, dst_ref=dst, send_sem=send, recv_sem=recv, device_id=device, device_id_type=MESH
    )
    copy.start()
    return copy


def line_partners(n, xyz, core):
    for axis in range(3):
        for k in range(1, n):
            for dc in range(2):
                yield device_of(n, moved(n, xyz, axis, k), lax.rem(core + dc, 2))
    yield device_of(n, xyz, 1 - core)


def partners(n, xyz, core):
    yield from line_partners(n, xyz, core)
    for dy in range(1, n):
        for dz in range(1, n):
            yield device_of(n, moved(n, moved(n, xyz, 1, dy), 2, dz), core)


def split(value):
    high = value.astype(BF)
    return high, (value - high.astype(F32)).astype(BF)


def dot(a, b):
    return jnp.dot(a, b, preferred_element_type=F32)


def column(row):
    return jnp.broadcast_to(row, (row.shape[1], row.shape[1])).T


def kernel(
    n, rows, ids_ref, prior_ref, corr_ref, weight_ref, control_hbm, foot_hbm, obs_hbm,
    out_hbm,
    g00, g01, g02, g03, g10, g11, g12, g13, g20, g21, g22, g23,
    s0, s1, s2, b0, b1, b2, a0, a1, a2, h0, h1, h2, r0, r1, r2, m0, m1, m2, o0, o1, o2,
    foot, control, obs, out, weights, mismatch, mine, row_ids, table, table_t, pair_v, prev_v, last_v,
    table_s, pair_s, prev_s, last_s,
    load_sem, id_send, id_recv, scalar_sem, one_send, one_recv, two_send, two_recv, three_send, three_recv, keep_sem,
    back_three_send, back_three_recv, back_keep_sem, back_two_send, back_two_recv, back_one_send, back_one_recv,
    out_sem, free_sem,
):
    gathered = ((g00, g01, g02, g03), (g10, g11, g12, g13), (g20, g21, g22, g23))
    picked, middle, arrived = (s0, s1, s2), (b0, b1, b2), (a0, a1, a2)
    chain, sums_in, relay, own = (h0, h1, h2), (r0, r1, r2), (m0, m1, m2), (o0, o1, o2)
    tiles, cells, members = control.shape
    blocks, touched = ids_ref.shape
    per_block = foot.shape[1]
    xyz, core = here(n)
    starts = part_starts(cells)
    lanes = 2 * n * n * n
    none = 2 * n * n
    half = tiles // 2
    halves = (pl.ds(0, half), pl.ds(half, half))

    barrier = pltpu.get_barrier_semaphore()
    count = 0
    for target in partners(n, xyz, core):
        pl.semaphore_signal(barrier, inc=1, device_id=target, device_id_type=MESH)
        count += 1

    loads = []
    for i, (src, dst) in enumerate(((control_hbm, control), (foot_hbm, foot), (obs_hbm, obs))):
        loads.append(pltpu.make_async_copy(src, dst, load_sem.at[i]))
        loads[-1].start()
    load_control, load_foot, load_obs = loads

    lane = lax.broadcasted_iota(I32, (8, lanes), 1)
    wanted = jnp.full((8, lanes), tiles, I32)
    pair = jnp.zeros((8, lanes), I32)
    for b in range(blocks):
        for k in range(touched):
            tile = ids_ref[b, k]
            match = lane == lax.div(tile, tiles)
            wanted = jnp.where(match, lax.rem(tile, tiles), wanted)
            pair = jnp.where(match, b * touched + k, pair)
    pair_v[...] = pair
    mine[...] = wanted
    me = xyz[0] * 2 + core
    row_ids[pl.ds(me, 1)] = wanted[None]
    to_scalar = [pltpu.make_async_copy(pair_v, pair_s, scalar_sem.at[0])]
    to_scalar[0].start()

    corr_h, corr_l = split(corr_ref[...])
    load_control.wait()

    def emit(i, carry):
        t = 2 * i
        both = jnp.concatenate([control[t], control[t + 1]], axis=1)
        both_h, both_l = split(both)
        flux = dot(corr_h, both_h) + (dot(corr_h, both_l) + dot(corr_l, both_h))
        for u in range(2):
            prior = prior_ref[pl.ds(t + u, 1), :]
            base = jnp.concatenate(
                [column(prior[:, members * v : members * (v + 1)]) for v in range(cells // members)], axis=0
            )
            tile = (base + flux[:, members * u : members * (u + 1)]).astype(BF)
            for p in range(3):
                gathered[p][0][t + u] = tile[starts[p] : starts[p] + rows[p]]
        return carry

    lax.fori_loop(0, tiles // 2, emit, 0)

    pl.semaphore_wait(barrier, count)

    sent = []
    row_copies = []
    for dx in range(n):
        for dc in range(2):
            if dx or dc:
                target = device_of(n, moved(n, xyz, 0, dx), lax.rem(core + dc, 2))
                i = dx * 2 + dc
                row_copies.append(remote(mine, row_ids.at[me], id_send.at[i], id_recv.at[i], target))
    sent += row_copies

    one = {}

    def gather(p, k, j, h):
        i = (p * n + (j - k) % n) * 2 + h
        one[p, (j - k) % n, h] = remote(
            gathered[p][j].at[halves[h]], gathered[p][(j - k) % n].at[halves[h]], one_send.at[i], one_recv.at[i],
            device_of(n, moved(n, xyz, ORDERS[p][0], k), core),
        )
        sent.append(one[p, (j - k) % n, h])

    for p in range(3):
        gather(p, 3, 0, 0)
        gather(p, 1, 0, 1)

    for copy in row_copies:
        copy.wait_recv()
    for e in range(2 * n):
        table[xyz[2], xyz[1], e : e + 1, :] = row_ids[e, 0:1, :]
    plane_copies = []
    at = 2 * n
    for dy in range(n):
        for dz in range(n):
            if dy or dz:
                target = device_of(n, moved(n, moved(n, xyz, 1, dy), 2, dz), core)
                i = at + dy * n + dz
                here_ids = table.at[xyz[2], xyz[1]]
                plane_copies.append(remote(here_ids, here_ids, id_send.at[i], id_recv.at[i], target))
    sent += plane_copies

    for p in range(3):
        gather(p, 3, 0, 1)
        gather(p, 1, 0, 0)
    for p in range(3):
        one[p, 1, 0].wait_recv()
        gather(p, 3, 1, 0)
        one[p, 3, 1].wait_recv()
        gather(p, 1, 3, 1)

    for copy in plane_copies:
        copy.wait_recv()
    table_copy = pltpu.make_async_copy(table, table_s, scalar_sem.at[1])
    table_copy.start()
    table_copy.wait()

    two = {}
    for j in (0,) + STEPS:
        for p in range(3):
            if j == 2:
                one[p, 2, 0].wait_recv()
                one[p, 2, 1].wait_recv()
            elif j:
                one[p, j, 1 if j == 1 else 0].wait_recv()
        for kk, k in enumerate(STEPS + (0,)):
            for p, (first, second, third) in enumerate(ORDERS):
                source = lax.rem(xyz[first] + j, n)
                owner = owner_of(n, placed(xyz, first, source), core)
                column_at = moved(n, xyz, second, k)

                def pick(d, carry, p=p, j=j, k=k, kk=kk, third=third, column_at=column_at, owner=owner, source=source,
                         second=second):
                    x, y, z = placed(column_at, third, lax.rem(d, n))
                    tile = table_s[z, y, x * 2 + lax.rem(core + lax.div(d, n), 2), owner]
                    value = gathered[p][j][jnp.clip(tile, 0, tiles - 1)]
                    if k:
                        picked[p][kk, j, d] = value
                    else:
                        middle[p][d, xyz[second], source] = value
                    return carry

                lax.fori_loop(0, 2 * n, pick, 0)
                if k:
                    for other in range(2):
                        i = ((p * n + k) * n + j) * 2 + other
                        span, at_rows = pl.ds(other * n, n), sent_rows(rows, p, other)
                        two[p, k, j, other] = remote(
                            picked[p].at[kk, j, span, at_rows], middle[p].at[span, xyz[second], source, at_rows],
                            two_send.at[i], two_recv.at[i], device_of(n, column_at, core),
                        )
                        sent.append(two[p, k, j, other])

    final = []
    kept = []
    for k in (0,) + STEPS:
        if k:
            for p in range(3):
                for j in range(n):
                    for other in range(2):
                        two[p, k, j, other].wait_recv()
        for ds in STEPS + (0,):
            for other in range(2):
                for p, (first, second, third) in enumerate(ORDERS):
                    source = lax.rem(xyz[second] + n - k, n)
                    mine_at = other * n + xyz[third]
                    at_rows = sent_rows(rows, p, other)
                    goal = moved(n, xyz, third, ds)
                    src = middle[p].at[other * n + goal[third], source, :, at_rows]
                    dst = arrived[p].at[mine_at, source, :, at_rows]
                    if ds or other:
                        i = ((p * n + k) * n + ds) * 2 + other
                        final.append(
                            remote(src, dst, three_send.at[i], three_recv.at[i],
                                   device_of(n, goal, lax.rem(core + other, 2)))
                        )
                    else:
                        kept.append(pltpu.make_async_copy(src, dst, keep_sem.at[p * n + k]))
                        kept[-1].start()
    table_t[...] = table[...].reshape(lanes, lanes).T
    shape = (lanes, lanes)
    coords = []
    for dim in range(2):
        r = lax.broadcasted_iota(I32, shape, dim)
        coords.append(
            ((lax.div(lax.rem(r, 2 * n), 2), lax.rem(lax.div(r, 2 * n), n), lax.div(r, 2 * n * n)), lax.rem(r, 2))
        )
    tile_at = lax.broadcasted_iota(I32, (tiles, lanes), 0)
    last_lane = lax.broadcasted_iota(I32, (tiles, lanes), 1)
    lasts = jnp.full((tiles, lanes), none, I32)
    prev_v[...] = jnp.zeros(prev_v.shape, I32)
    for p, (first, second, third) in enumerate(ORDERS):
        rank = [
            (lax.rem(c[second] + (n - xyz[second]), n) * n + c[third]) * 2 + lax.rem(o + core, 2)
            for c, o in coords
        ]
        in_plane = [c[first] == xyz[first] for c, o in coords]
        earlier = (rank[0] < rank[1]) & in_plane[0]
        for j in range(n):
            owner = owner_of(n, moved(n, xyz, first, j), core)
            across = jnp.broadcast_to(table_t[pl.ds(owner, 1), :], shape)
            down = across.T
            before = jnp.max(jnp.where(earlier & (across == down), rank[0], -1), axis=0, keepdims=True)
            prev_v[p * n + j : p * n + j + 1, :] = jnp.where(before < 0, none, before)
            hit = (across[:tiles] == tile_at) & in_plane[1][:tiles]
            newest = jnp.max(jnp.where(hit, rank[1][:tiles], -1), axis=1, keepdims=True)
            newest = jnp.where(newest < 0, none, newest)
            lasts = jnp.where(last_lane == p * n + j, newest, lasts)
    last_v[...] = lasts
    for i, (src, dst) in enumerate(((prev_v, prev_s), (last_v, last_s))):
        to_scalar.append(pltpu.make_async_copy(src, dst, scalar_sem.at[2 + i]))
        to_scalar[-1].start()
    for p in range(3):
        chain[p][none] = jnp.zeros((rows[p], members), F32)

    per = per_block // members
    for b in range(blocks):
        for v in range(per):
            weights[b, v * members : (v + 1) * members] = column(weight_ref[b * per + v : b * per + v + 1, :])

    load_foot.wait()
    load_obs.wait()
    for copy in to_scalar + kept:
        copy.wait()
    for copy in sent:
        copy.wait_send()
    per_step = len(final) // n
    for k in range(n):
        for copy in final[k * per_step : (k + 1) * per_step]:
            copy.wait_recv()
        for copy in final[k * per_step : (k + 1) * per_step]:
            copy.wait_send()
    freed = 0
    for target in line_partners(n, xyz, core):
        pl.semaphore_signal(free_sem, inc=1, device_id=target, device_id_type=MESH)
        freed += 1

    def model(b, carry):
        feet, flux = [], []
        for k in range(touched):
            tile = lax.div(ids_ref[b, k], tiles)
            oc = lax.rem(tile, 2)
            c = (lax.rem(lax.div(tile, 2), n), lax.div(tile, 2 * n * n), lax.rem(lax.div(tile, 2 * n), n))
            other = lax.rem(oc + core, 2)
            v0, v1, v2 = (
                arrived[p][other * n + c[third], c[second], c[first]]
                for p, (first, second, third) in enumerate(ORDERS)
            )
            shared = jnp.where(other == 0, v0[rows[0] - SHARED :], v1[:SHARED])
            flux += [v0[: rows[0] - SHARED], shared, v1[SHARED:], v2]
            feet.append(foot[b * touched + k])
        modeled = dot(jnp.concatenate(feet, axis=1), jnp.concatenate(flux, axis=0))
        wrong = (modeled - obs[pl.ds(pl.multiple_of(b * per_block, per_block), per_block), :]) * weights[b]
        mismatch[b] = wrong.T.astype(BF)
        return carry

    lax.fori_loop(0, blocks, model, 0, unroll=2)

    sent = []
    one_way = {}

    def give_back(turn, ds, other):
        for p, (first, second, third) in enumerate(ORDERS):
            goal = moved(n, xyz, third, ds)
            at_rows = sent_rows(rows, p, other)
            lies = (turn - ds) % n
            src = arrived[p].at[other * n + goal[third], lies, :, at_rows]
            dst = middle[p].at[other * n + xyz[third], lies, :, at_rows]
            if ds or other:
                i = ((p * n + turn) * n + ds) * 2 + other
                copy = remote(src, dst, back_three_send.at[i], back_three_recv.at[i],
                              device_of(n, goal, lax.rem(core + other, 2)))
                sent.append(copy)
            else:
                copy = pltpu.make_async_copy(src, dst, back_keep_sem.at[p * n + turn])
                copy.start()
            one_way.setdefault((p, lies), []).append((copy, bool(ds or other)))

    for turn in range(n):

        for other in range(2):

            def make(i, carry, turn=turn, other=other):
                dx, dy = lax.rem(i, n), lax.div(i, n)
                far = (dx, dy, lax.rem(turn + 2 * n - dx - dy, n))
                c = tuple(lax.rem(xyz[a] + far[a], n) for a in range(3))
                pair = jnp.clip(pair_s[0, owner_of(n, c, lax.rem(core + other, 2))], 0, blocks * touched - 1)
                value = dot(mismatch[lax.div(pair, touched)], foot[pair]).astype(BF).T
                for p, (first, second, third) in enumerate(ORDERS):
                    arrived[p][other * n + c[third], lax.rem(far[second] + far[first], n), c[second]] = (
                        value[starts[p] : starts[p] + rows[p]]
                    )
                return carry

            lax.fori_loop(0, n * n, make, 0, unroll=8)
            if turn == 0 and other == 0:
                pl.semaphore_wait(free_sem, freed)
            for ds in STEPS + (0,):
                if turn == 0 or ds == turn:
                    give_back(turn, ds, other)

    for turn in range(1, n):
        for other in range(2):
            for ds in STEPS + (0,):
                if ds != turn:
                    give_back(turn, ds, other)

    def arrive(first_lies):
        for (p, lies), copies in one_way.items():
            if (lies == 0) == first_lies:
                for copy, far in copies:
                    if far:
                        copy.wait_recv()
                    else:
                        copy.wait()

    two = {}

    def pass_on(j, steps):
        for k in steps:
            for p, (first, second, third) in enumerate(ORDERS):
                goal = moved(n, xyz, second, k)
                for other in range(2):
                    span, at_rows = pl.ds(other * n, n), sent_rows(rows, p, other)
                    i = ((p * n + k) * n + j) * 2 + other
                    two[p, k, j, other] = remote(
                        middle[p].at[span, (k + j) % n, goal[second], at_rows],
                        picked[p].at[STEPS.index(n - k), j, span, at_rows],
                        back_two_send.at[i], back_two_recv.at[i], device_of(n, goal, core),
                    )
                    sent.append(two[p, k, j, other])

    arrive(True)
    for j in BACK:
        pass_on(j, (n - j,))
    arrive(False)
    for j in BACK:
        pass_on(j, [k for k in STEPS if k != n - j])

    one = {}
    relayed = {}

    def give(p, k, j, h, key, src, dst, i):
        copy = remote(
            src, dst, back_one_send.at[i], back_one_recv.at[i],
            device_of(n, moved(n, xyz, ORDERS[p][0], k), core),
        )
        sent.append(copy)
        return copy

    for j in BACK + (0,):
        if j == 1:
            pass_on(0, STEPS)
        for p in (1, 2, 0):
            first, second, third = ORDERS[p]
            for k in STEPS:
                for other in range(2):
                    two[p, k, j, other].wait_recv()
            for step in range(n):

                def link(third_at, carry, p=p, j=j, first=first, second=second, third=third, step=step):
                    so = lax.rem(xyz[second] + step, n)
                    c = placed(placed(xyz, second, so), third, third_at)
                    for other in range(2):
                        d = other * n + third_at
                        device = (c[2] * n + c[1]) * (2 * n) + c[0] * 2 + lax.rem(core + other, 2)
                        before = jnp.clip(prev_s[p * n + j, device], 0, none)
                        at = sent_rows(rows, p, other)
                        if step:
                            value = picked[p][STEPS.index(step), j, d, at]
                        else:
                            value = middle[p][d, j, so, at]
                        chain[p][(step * n + third_at) * 2 + other, at] = value.astype(F32) + chain[p][before, at]
                        if at.size < rows[p]:
                            rest = pl.ds(at.size if at.start == 0 else 0, rows[p] - at.size)
                            chain[p][(step * n + third_at) * 2 + other, rest] = chain[p][before, rest]
                    return carry

                lax.fori_loop(0, n, link, 0, unroll=2)

            for h in range(2):
                joins = (j == 1 and h == 0) or (j == 3 and h == 1)
                if joins:
                    relayed[p, h].wait_recv()

                def collect(t, carry, p=p, j=j, h=h, joins=joins):
                    total = chain[p][jnp.clip(last_s[h * half + t, p * n + j], 0, none)]
                    if joins:
                        total = total + relay[p][h, t].astype(F32)
                    if j:
                        gathered[p][j][h * half + t] = total.astype(BF)
                    else:
                        own[p][h * half + t] = total
                    return carry

                lax.fori_loop(0, half, collect, 0, unroll=4)
                if j == 2:
                    k = 1 if h == 0 else 3
                    relayed[p, h] = give(
                        p, k, j, h, "relay", gathered[p][j].at[halves[h]], relay[p].at[h], (p * n + 2) * 2 + h
                    )
                elif j:
                    one[p, j, h] = give(
                        p, j, j, h, "sum", gathered[p][j].at[halves[h]],
                        sums_in[p].at[0 if j == 1 else 1, halves[h]], (p * n + j) * 2 + h,
                    )

    corr_h, corr_l = split(corr_ref[...].T)
    late = list(one.values())
    for copy in sent:
        if all(copy is not other for other in late):
            copy.wait_send()
    stores = []
    for h in range(2):
        for p in (1, 2, 0):
            for j in (1, 3):
                one[p, j, h].wait_recv()

        def finish(i, carry, h=h):
            t = h * half + 2 * i
            adjoint = []
            for u in range(2):
                v0, v1, v2 = (
                    own[p][t + u] + (sums_in[p][0, t + u].astype(F32) + sums_in[p][1, t + u].astype(F32))
                    for p in range(3)
                )
                shared = v0[rows[0] - SHARED :] + v1[:SHARED]
                adjoint.append(jnp.concatenate([v0[: rows[0] - SHARED], shared, v1[SHARED:], v2], axis=0))
            both_h, both_l = split(jnp.concatenate(adjoint, axis=1))
            spread = dot(corr_h, both_h) + (dot(corr_h, both_l) + dot(corr_l, both_h))
            for u in range(2):
                out[t + u] = control[t + u] + spread[:, members * u : members * (u + 1)]
            return carry

        lax.fori_loop(0, half // 2, finish, 0, unroll=2)
        stores.append(pltpu.make_async_copy(out.at[halves[h]], out_hbm.at[halves[h]], out_sem.at[h]))
        stores[-1].start()

    for copy in late:
        copy.wait_send()
    for copy in stores:
        copy.wait()


def per_device(n, control, prior_flux, correlation, footprints, obs_values, obs_weights, tile_ids):
    tiles, cells, members = control.shape
    blocks, touched = tile_ids.shape
    per_block = footprints.shape[2]
    owners = 2 * n * n * n
    rows = part_rows(cells)
    foot = footprints.reshape(blocks * touched, per_block, cells)
    vmem, smem, anywhere = (
        pl.BlockSpec(memory_space=pltpu.VMEM),
        pl.BlockSpec(memory_space=pltpu.SMEM),
        pl.BlockSpec(memory_space=pl.ANY),
    )

    def dma(count):
        return pltpu.SemaphoreType.DMA((count,))

    return pl.pallas_call(
        functools.partial(kernel, n, rows),
        name="gradient",
        out_shape=jax.ShapeDtypeStruct(control.shape, F32),
        in_specs=[smem, vmem, vmem, vmem, anywhere, anywhere, anywhere],
        out_specs=anywhere,
        scratch_shapes=(
            [pltpu.VMEM((tiles, r, members), BF) for r in rows for _ in range(4)]
            + [pltpu.VMEM((n - 1, n, 2 * n, r, members), BF) for r in rows]
            + [pltpu.VMEM((2 * n, n, n, r, members), BF) for r in rows]
            + [pltpu.VMEM((2 * n, n, n, r, members), BF) for r in rows]
            + [pltpu.VMEM((2 * n * n + 1, r, members), F32) for r in rows]
            + [pltpu.VMEM((2, tiles, r, members), BF) for r in rows]
            + [pltpu.VMEM((2, tiles // 2, r, members), BF) for r in rows]
            + [pltpu.VMEM((tiles, r, members), F32) for r in rows]
            + [
                pltpu.VMEM((blocks * touched, per_block, cells), BF),
                pltpu.VMEM(control.shape, F32),
                pltpu.VMEM(obs_values.shape, F32),
                pltpu.VMEM(control.shape, F32),
                pltpu.VMEM((blocks, per_block, members), F32),
                pltpu.VMEM((blocks, members, per_block), BF),
                pltpu.VMEM((8, owners), I32),
                pltpu.VMEM((2 * n, 8, owners), I32),
                pltpu.VMEM((n, n, 2 * n, owners), I32),
                pltpu.VMEM((owners, owners), I32),
                pltpu.VMEM((8, owners), I32),
                pltpu.VMEM((16, owners), I32),
                pltpu.VMEM((tiles, owners), I32),
                pltpu.SMEM((n, n, 2 * n, owners), I32),
                pltpu.SMEM((8, owners), I32),
                pltpu.SMEM((16, owners), I32),
                pltpu.SMEM((tiles, owners), I32),
                dma(3), dma(2 * n + n * n), dma(2 * n + n * n), dma(4),
                dma(6 * n), dma(6 * n),
                dma(6 * n * n), dma(6 * n * n),
                dma(6 * n * n), dma(6 * n * n), dma(3 * n),
                dma(6 * n * n), dma(6 * n * n), dma(3 * n),
                dma(6 * n * n), dma(6 * n * n),
                dma(6 * n), dma(6 * n),
                dma(2), pltpu.SemaphoreType.REGULAR,
            ]
        ),
        compiler_params=pltpu.CompilerParams(
            collective_id=0, has_side_effects=True, vmem_limit_bytes=VMEM_BYTES
        ),
    )(tile_ids, prior_flux, correlation, obs_weights.reshape(-1, members), control, foot, obs_values)


def solution(mesh):
    n = mesh.shape["emis"] // 2
    return jax.shard_map(
        functools.partial(per_device, n),
        mesh=mesh,
        in_specs=(
            P(("obs", "emis"), None, None),
            P(("obs", "emis"), None),
            P(),
            P(("obs", "emis"), None, None, None),
            P(("obs", "emis"), None),
            P(("obs", "emis")),
            P(("obs", "emis"), None),
        ),
        out_specs=P(("obs", "emis"), None, None),
        check_vma=False,
    )
```
